32 devices in a mesh: grp: 4 (over z), exp: 4 (over y, core), rep: 2 (over x).
Axes of the slice: x: 2, y: 2, z: 4, core: 2. Of those that a mesh axis runs over, the one named last changes fastest.
Arguments:
- tokens: bfloat16 [512, 2048], P(('rep', 'grp', 'exp')), parts along dimension 0, may hold values from -6 to 6
- expert_ids: int32 [512, 8], P(('rep', 'grp', 'exp')), parts along dimension 0, may hold values from 0 to 15, as said below
- gate_weights: bfloat16 [512, 8], P(('rep', 'grp', 'exp')), parts along dimension 0, may hold values from 0.049804688 to 0.3984375
- w_gate: bfloat16 [16, 2048, 768], P(('grp', 'exp')), may hold values from -0.125 to 0.125
- w_up: bfloat16 [16, 2048, 768], P(('grp', 'exp')), may hold values from -0.125 to 0.125
- w_down: bfloat16 [16, 768, 2048], P(('grp', 'exp')), may hold values from -0.21875 to 0.21875
Outputs:
- combined: float32 [512, 2048], P(('rep', 'grp', 'exp')), parts along dimension 0
The draws below stay inside these ranges and needn't reach their ends.
There are 2 independent parts, one for each index of `rep`. The reference program is written for one: setup_inputs(seed, part) draws one part's arguments, and reference() takes and returns one part's arrays. A program takes and returns all parts, laid end to end along the dimension named above; an argument that names none is the same for every part. Nothing has to cross between parts.
Inputs may be any that keep to these rules, and one draw needn't show every extreme that they name: `expert_ids`: expert x belongs to group x // 4. Each row names 8 different experts, 4 of them in each of two different groups. Of the 16 rows of one device (aligned blocks of 16 rows), at most 16 name experts of any one group and at most 16 name any one expert; in every draw one group is named by 16 rows of every device, and each of its experts by 16 rows of every device.
All inputs are finite; a program needn't handle non-finite values.
Results may differ from the reference program's by a relative error of at most 0.0041.
Values may be sent and summed in bfloat16 or wider, within the bound.
No kernel may reach another device: no remote copies, remote signals or barrier semaphores. Data moves between devices by JAX's collectives and lax.ppermute only.
A program may use at most 64 MiB of HBM per device.

```python
from functools import partial
import jax
import jax.numpy as jnp
from jax import lax

D = 2048
FF = 768
TOP = 8
PER_GROUP = 4
TOK_DEV = 16
GROUPS = 4
GRP_EXPERTS = 4
EXPERTS = 16
TOKENS = 256
CAP_GRP = 16
CAP_EXP = 16


def pick_index(pick_key, eligible):
    priority = jax.random.randint(pick_key, eligible.shape, 0, 1 << 20)
    return jnp.argmax(jnp.where(eligible, priority, -1)).astype(jnp.int32)


def shuffle_row(row_key, id_row):
    return jax.random.permutation(row_key, id_row)


def group_order(group_key):
    return jax.random.permutation(group_key, GRP_EXPERTS)


def device_routes(device_key, busiest):
    mean_load = 2 * TOK_DEV // GROUPS
    group_grid = jnp.arange(GROUPS, dtype=jnp.int32)
    counts = jnp.full((GROUPS,), mean_load, jnp.int32).at[busiest].set(CAP_GRP)

    def lower_one(step_index, counts):
        eligible = (counts > 0) & (group_grid != busiest)
        chosen = pick_index(jax.random.fold_in(device_key, step_index), eligible)
        return counts.at[chosen].add(-1)
    counts = lax.fori_loop(0, CAP_GRP - mean_load, lower_one, counts)

    def shuffle(step_index, counts):
        source = pick_index(jax.random.fold_in(device_key, 1000 + step_index), (counts > 0) & (group_grid != busiest))
        target = pick_index(jax.random.fold_in(device_key, 5000 + step_index), (counts < CAP_GRP - 1) & (group_grid != busiest) & (group_grid != source))
        shifted = counts.at[source].add(-1).at[target].add(1)
        allowed = (counts[source] > 0) & (counts[target] < CAP_GRP - 1) & (source != target) & (source != busiest) & (target != busiest)
        return jnp.where(allowed, shifted, counts)
    counts = lax.fori_loop(0, 2 * GROUPS, shuffle, counts)
    run_ends = jnp.cumsum(counts)
    starts = run_ends - counts
    positions = jnp.arange(2 * TOK_DEV, dtype=jnp.int32)
    labels = jnp.sum((run_ends[None, :] <= positions[:, None]).astype(jnp.int32), axis=1)
    rank_in_group = positions - starts[labels]
    orders = jax.vmap(group_order)(jax.random.split(jax.random.fold_in(device_key, 9000), GROUPS))
    spot_index = PER_GROUP * rank_in_group[:, None] + jnp.arange(PER_GROUP, dtype=jnp.int32)[None, :]
    local_ids = orders[labels[:, None], spot_index % GRP_EXPERTS]
    chosen_ids = labels[:, None] * GRP_EXPERTS + local_ids
    id_rows = jnp.concatenate([chosen_ids[:TOK_DEV], chosen_ids[TOK_DEV:]], axis=1)
    id_rows = jax.vmap(shuffle_row)(jax.random.split(jax.random.fold_in(device_key, 9100), TOK_DEV), id_rows)
    id_rows = jax.random.permutation(jax.random.fold_in(device_key, 9200), id_rows, axis=0)
    return id_rows.astype(jnp.int32)


def draw_expert_ids(key, part):
    busiest = jax.random.randint(jax.random.fold_in(key, 7), (), 0, GROUPS).astype(jnp.int32)
    device_keys = jax.random.split(jax.random.fold_in(key, 8), GROUPS * GRP_EXPERTS)
    all_devices = jax.vmap(partial(device_routes, busiest=busiest))(device_keys)
    return all_devices.reshape(TOKENS, TOP)


def levels(own_key, shape, cuts, low, largest):
    factor_of, own = 1.0, jax.random.fold_in(own_key, 6)
    for dim, parts in cuts:
        heights = jnp.exp(jax.random.uniform(jax.random.fold_in(own, dim), (parts,), jnp.float32, low / len(cuts), largest / len(cuts)))
        factor_of = factor_of * jnp.repeat(heights, shape[dim] // parts).reshape([-1 if axis == dim else 1 for axis in range(len(shape))])
    return factor_of


def gaussian(key, shape, scale, bound, cuts=(), kind=jnp.bfloat16):
    result = scale * jax.random.normal(key, shape, jnp.float32)
    if cuts:
        result = result * levels(key, shape, cuts, -0.22, 0.18)
    return jnp.clip(result, -bound, bound).astype(kind)


def setup_inputs(seed: int = 0, part: int = 0) -> dict:
    seeds = jax.random.split(jax.random.key(seed), 7)
    own_keys = jax.random.split(jax.random.fold_in(seeds[6], part), 7)
    return {
        "tokens": gaussian(own_keys[0], (TOKENS, D), 1.0, 6.0, ((0, 16),)),
        "expert_ids": draw_expert_ids(jax.random.fold_in(jax.random.fold_in(seeds[6], part), 71), part),
        "gate_weights": jnp.clip(0.049804688 + 0.3486328 * jax.random.uniform(own_keys[2], (TOKENS, TOP), jnp.float32) ** levels(own_keys[2], (TOKENS, TOP), ((0, 16),), -0.2, 0.2), 0.049804688, 0.3984375).astype(jnp.bfloat16),
        "w_gate": gaussian(seeds[3], (EXPERTS, D, FF), D ** -0.5, 0.125, ((0, 16),)),
        "w_up": gaussian(seeds[4], (EXPERTS, D, FF), D ** -0.5, 0.125, ((0, 16),)),
        "w_down": gaussian(seeds[5], (EXPERTS, FF, D), FF ** -0.5, 0.21875, ((0, 16),)),
    }


def expert_apply(token_rows, gate_mat, up_mat, down_mat):
    gate_pre = jnp.dot(token_rows, gate_mat, preferred_element_type=jnp.float32)
    up_pre = jnp.dot(token_rows, up_mat, preferred_element_type=jnp.float32)
    hidden = (jax.nn.silu(gate_pre) * up_pre).astype(jnp.bfloat16)
    return jnp.dot(hidden, down_mat, preferred_element_type=jnp.float32).astype(jnp.bfloat16)


def reference(tokens, expert_ids, gate_weights, w_gate, w_up, w_down):
    flat_ids = expert_ids.reshape(-1)
    flat_gates = gate_weights.reshape(-1).astype(jnp.float32)
    capacity = GROUPS * GRP_EXPERTS * CAP_EXP

    def visit_expert(running, expert):
        chosen = flat_ids == expert
        ordering = jnp.argsort(jnp.where(chosen, 0, 1).astype(jnp.int32), stable=True)[:capacity]
        row_index = (ordering // TOP).astype(jnp.int32)
        outputs = expert_apply(tokens[row_index], w_gate[expert], w_up[expert], w_down[expert])
        weights = jnp.where(chosen[ordering], flat_gates[ordering], jnp.zeros((), jnp.float32))
        running = running.at[row_index].add(weights[:, None] * outputs.astype(jnp.float32))
        return running, None

    running, unused = lax.scan(visit_expert, jnp.zeros((TOKENS, D), jnp.float32), jnp.arange(EXPERTS, dtype=jnp.int32))
    return running
```

```python
import jax
import jax.numpy as jnp
from jax import lax
from jax.sharding import PartitionSpec as P


def shards(tokens, expert_ids, gate_weights, w_gate, w_up, w_down):
    tok_rows, model_width = tokens.shape
    owners = lax.axis_size("exp")
    experts = lax.axis_size("grp") * owners
    mine = lax.axis_index("grp") * owners + lax.axis_index("exp")
    expert_grid = jnp.arange(experts, dtype=jnp.int32)
    chosen = expert_ids[:, :, None] == expert_grid
    zero = jnp.zeros((), jnp.bfloat16)
    table = jnp.sum(jnp.where(chosen, gate_weights[:, :, None], zero), axis=1)
    rows = lax.all_gather(tokens, ("grp", "exp"), axis=0, tiled=True)
    tables = lax.all_gather(table, ("grp", "exp"), axis=0, tiled=True)
    gate_pre = jnp.dot(rows, w_gate[0], preferred_element_type=jnp.float32)
    up_pre = jnp.dot(rows, w_up[0], preferred_element_type=jnp.float32)
    hidden = (jax.nn.silu(gate_pre) * up_pre).astype(jnp.bfloat16)
    result = jnp.dot(hidden, w_down[0], preferred_element_type=jnp.float32)
    scale = jnp.sum(jnp.where(expert_grid == mine, tables.astype(jnp.float32), 0.0), axis=1)
    part = (result * scale[:, None]).astype(jnp.bfloat16)
    return lax.psum_scatter(part, ("grp", "exp"), scatter_dimension=0, tiled=True).astype(jnp.float32)


def solution(mesh):
    return jax.shard_map(
        shards,
        mesh=mesh,
        in_specs=(
            P(("rep", "grp", "exp"), None),
            P(("rep", "grp", "exp"), None),
            P(("rep", "grp", "exp"), None),
            P(("grp", "exp"), None, None),
            P(("grp", "exp"), None, None),
            P(("grp", "exp"), None, None),
        ),
        out_specs=P(("rep", "grp", "exp"), None),
        check_vma=False,
    )
```

```python
import functools

import jax
import jax.numpy as jnp
from jax import lax
from jax.experimental import pallas as pl
from jax.experimental.pallas import tpu as pltpu
from jax.sharding import PartitionSpec as P

CORES = 2
WHOLE_ROWS = 512


def partner(index, step, count):
    return index ^ step if count & (count - 1) == 0 else (index + step) % count


def move(value, axis, pairs, back):
    return lax.ppermute(value, axis, [(d, s) for s, d in pairs] if back else pairs)


def expert_kernel(rows, mine_ref, x_ref, gate_ref, up_ref, down_ref, out_ref):
    model_width = out_ref.shape[1]

    def body(step, carry):
        part = pl.ds(pl.multiple_of(step * rows, rows), rows)
        x = x_ref[part, :model_width]
        table = x_ref[part, model_width:].astype(jnp.float32)
        lane = lax.broadcasted_iota(jnp.int32, table.shape, 1)
        scale = jnp.sum(jnp.where(lane == mine_ref[0], table, 0.0), axis=1, keepdims=True)
        gate_pre = jnp.dot(x, gate_ref[0], preferred_element_type=jnp.float32)
        up_pre = jnp.dot(x, up_ref[0], preferred_element_type=jnp.float32)
        hidden = (gate_pre / (1.0 + jnp.exp(-gate_pre)) * up_pre).astype(jnp.bfloat16)
        result = jnp.dot(hidden, down_ref[0], preferred_element_type=jnp.float32)
        out_ref[part, :] = (result * scale).astype(out_ref.dtype)
        return carry

    lax.fori_loop(0, x_ref.shape[0] // rows, body, 0)


def expert_rows(mine, model_width, w_gate, w_up, w_down, x, out_type):
    total = x.shape[0]
    rows = total if total <= 256 else 256
    in_vmem = pl.BlockSpec(memory_space=pltpu.VMEM)
    hidden_width = w_gate.shape[2]
    return pl.pallas_call(
        functools.partial(expert_kernel, rows),
        out_shape=jax.ShapeDtypeStruct((total, model_width), out_type),
        in_specs=[pl.BlockSpec(memory_space=pltpu.SMEM)] + [in_vmem] * 4,
        out_specs=in_vmem,
        compiler_params=pltpu.CompilerParams(vmem_limit_bytes=24 << 20),
        cost_estimate=pl.CostEstimate(
            flops=6 * total * model_width * hidden_width,
            bytes_accessed=6 * model_width * hidden_width,
            transcendentals=total * hidden_width,
        ),
    )(mine, x, w_gate, w_up, w_down)


def shards(tokens, expert_ids, gate_weights, w_gate, w_up, w_down):
    tok_rows, model_width = tokens.shape
    groups = lax.axis_size("grp")
    owners = lax.axis_size("exp")
    experts = groups * owners
    chips = owners // CORES
    mine = lax.axis_index("grp") * owners + lax.axis_index("exp")

    def along_grp(value, step, back=False):
        return move(value, "grp", [(i, partner(i, step, groups)) for i in range(groups)], back)

    def along_chip(value, step, back=False):
        pairs = [
            (i * CORES + c, partner(i, step, chips) * CORES + c)
            for i in range(chips)
            for c in range(CORES)
        ]
        return move(value, "exp", pairs, back)

    def along_core(value):
        return move(value, "exp", [(i, i ^ 1) for i in range(owners)], False)

    expert_grid = jnp.arange(experts, dtype=jnp.int32)
    chosen = expert_ids[:, :, None] == expert_grid
    zero = jnp.zeros((), jnp.bfloat16)
    table = jnp.sum(jnp.where(chosen, gate_weights[:, :, None], zero), axis=1)
    table = jnp.pad(table, ((0, 0), (0, -experts % 128)))
    own = jnp.concatenate([tokens, table], axis=1)
    apply = functools.partial(expert_rows, mine[None], model_width, w_gate, w_up, w_down)
    width = groups if experts * tok_rows <= WHOLE_ROWS else 1
    total = jnp.zeros((tok_rows, model_width), jnp.float32)

    def narrow(value):
        return value.astype(jnp.bfloat16)

    for first in range(0, groups, width):
        if first:
            own, total = lax.optimization_barrier((own, total))
        steps = range(first, first + width)
        line = [along_grp(own, g) if g else own for g in steps]
        plane = [along_chip(piece, s) if s else piece for piece in line for s in range(chips)]
        block = jnp.concatenate(plane, axis=0)
        other = along_core(block)
        back = along_core(apply(other, jnp.bfloat16))
        both = apply(block, jnp.float32) + back.astype(jnp.float32)
        both = both.reshape(width, chips, tok_rows, model_width)
        for at, g in reversed(list(enumerate(steps))):
            piece = both[at, 0]
            for s in range(1, chips):
                piece = piece + along_chip(narrow(both[at, s]), s, True).astype(jnp.float32)
            if g:
                piece = along_grp(narrow(piece), g, True).astype(jnp.float32)
            total = total + piece
    return total


def solution(mesh):
    return jax.shard_map(
        shards,
        mesh=mesh,
        in_specs=(
            P(("rep", "grp", "exp"), None),
            P(("rep", "grp", "exp"), None),
            P(("rep", "grp", "exp"), None),
            P(("grp", "exp"), None, None),
            P(("grp", "exp"), None, None),
            P(("grp", "exp"), None, None),
        ),
        out_specs=P(("rep", "grp", "exp"), None),
        check_vma=False,
    )
```

```python
import functools

import jax
import jax.numpy as jnp
from jax import lax
from jax.experimental import pallas as pl
from jax.experimental.pallas import tpu as pltpu
from jax.sharding import PartitionSpec as P

CORES = 2
LANES = 128
WHOLE_ROWS = 512
VMEM = pl.BlockSpec(memory_space=pltpu.VMEM)
SMEM = pl.BlockSpec(memory_space=pltpu.SMEM)
HBM = pl.BlockSpec(memory_space=pltpu.HBM)


def partner(index, step, count):
    return index ^ step if count & (count - 1) == 0 else (index + step) % count


def move(value, axis, pairs, back):
    return lax.ppermute(value, axis, [(d, s) for s, d in pairs] if back else pairs)


def prep_kernel(ids_ref, gates_ref, tokens_ref, out_ref, ids_held, gates_held, sems):
    model_width = tokens_ref.shape[1]
    copies = [
        pltpu.make_async_copy(ids_ref, ids_held, sems.at[0]),
        pltpu.make_async_copy(gates_ref, gates_held, sems.at[1]),
        pltpu.make_async_copy(tokens_ref, out_ref.at[:, :model_width], sems.at[2]),
    ]
    for copy in copies:
        copy.start()
    copies[0].wait()
    copies[1].wait()
    width = out_ref.shape[1] - model_width
    top_count, rows = ids_held.shape
    ids = ids_held[...]
    gates = gates_held[...].astype(jnp.float32)
    expert = lax.broadcasted_iota(jnp.int32, (width, rows), 0)
    turned = jnp.zeros((width, rows), jnp.float32)
    for k in range(top_count):
        turned += jnp.where(ids[k : k + 1, :] == expert, gates[k : k + 1, :], 0.0)
    same = lax.broadcasted_iota(jnp.int32, (rows, rows), 0) == lax.broadcasted_iota(
        jnp.int32, (rows, rows), 1
    )
    table = lax.dot_general(
        same.astype(jnp.bfloat16),
        turned.astype(jnp.bfloat16),
        (((1,), (1,)), ((), ())),
        preferred_element_type=jnp.float32,
    )
    out_ref[:, model_width:] = table.astype(jnp.bfloat16)
    copies[2].wait()


def prepare(tokens, expert_ids, gate_weights, experts):
    rows, model_width = tokens.shape
    top_count = expert_ids.shape[1]
    width = experts + -experts % LANES
    return pl.pallas_call(
        prep_kernel,
        out_shape=jax.ShapeDtypeStruct((rows, model_width + width), jnp.bfloat16),
        in_specs=[HBM] * 3,
        out_specs=VMEM,
        scratch_shapes=[
            pltpu.VMEM((top_count, rows), jnp.int32),
            pltpu.VMEM((top_count, rows), jnp.bfloat16),
            pltpu.SemaphoreType.DMA((3,)),
        ],
        compiler_params=pltpu.CompilerParams(vmem_limit_bytes=8 << 20),
    )(expert_ids.T, gate_weights.T, tokens)


def load_kernel(parts, rows_ref, *refs):
    sems = refs[-1]
    count = (len(refs) - 2) // 2
    copies = [pltpu.make_async_copy(rows_ref, refs[count], sems.at[count * parts])]
    for at in range(count):
        source, target = refs[at].at[0], refs[count + 1 + at]
        rows = target.shape[0] // parts
        for part in range(parts):
            piece = pl.ds(part * rows, rows)
            copies.append(
                pltpu.make_async_copy(source.at[piece], target.at[piece], sems.at[at * parts + part])
            )
    for copy in copies:
        copy.start()
    for copy in copies:
        copy.wait()


def load_weights(rows, *weights):
    parts = 4
    out = [rows] + [jax.ShapeDtypeStruct(w.shape[1:], w.dtype) for w in weights]
    return pl.pallas_call(
        functools.partial(load_kernel, parts),
        out_shape=[jax.ShapeDtypeStruct(o.shape, o.dtype) for o in out],
        in_specs=[VMEM] + [HBM] * len(weights),
        out_specs=[VMEM] * len(out),
        scratch_shapes=[pltpu.SemaphoreType.DMA((parts * len(weights) + 1,))],
        compiler_params=pltpu.CompilerParams(vmem_limit_bytes=43 << 20),
        cost_estimate=pl.CostEstimate(
            flops=0, bytes_accessed=sum(w.size for w in weights) * 2, transcendentals=0
        ),
    )(rows, *weights)


def expert_kernel(rows, mine_ref, x_ref, gate_ref, up_ref, down_ref, out_ref):
    model_width = out_ref.shape[1]

    def body(step, carry):
        part = pl.ds(pl.multiple_of(step * rows, rows), rows)
        x = x_ref[part, :model_width]
        table = x_ref[part, model_width:].astype(jnp.float32)
        lane = lax.broadcasted_iota(jnp.int32, table.shape, 1)
        scale = jnp.sum(jnp.where(lane == mine_ref[0], table, 0.0), axis=1, keepdims=True)
        gate_pre = jnp.dot(x, gate_ref[...], preferred_element_type=jnp.float32)
        up_pre = jnp.dot(x, up_ref[...], preferred_element_type=jnp.float32)
        hidden = (gate_pre / (1.0 + jnp.exp(-gate_pre)) * up_pre).astype(jnp.bfloat16)
        result = jnp.dot(hidden, down_ref[...], preferred_element_type=jnp.float32)
        out_ref[part, :] = (result * scale).astype(out_ref.dtype)
        return carry

    lax.fori_loop(0, x_ref.shape[0] // rows, body, 0)


def expert_rows(mine, model_width, weights, x, out_type):
    total = x.shape[0]
    rows = next(r for r in range(min(total, 256), 0, -1) if total % r == 0)
    hidden_width = weights[0].shape[1]
    return pl.pallas_call(
        functools.partial(expert_kernel, rows),
        out_shape=jax.ShapeDtypeStruct((total, model_width), out_type),
        in_specs=[SMEM] + [VMEM] * 4,
        out_specs=VMEM,
        compiler_params=pltpu.CompilerParams(vmem_limit_bytes=16 << 20),
        cost_estimate=pl.CostEstimate(
            flops=6 * total * model_width * hidden_width,
            bytes_accessed=0,
            transcendentals=total * hidden_width,
        ),
    )(mine, x, *weights)


def add_kernel(first, *refs):
    out_ref = refs[-1]
    rows = out_ref.shape[0]
    total = None
    for ref in refs[:-1]:
        part = ref[...] if ref.shape[0] == rows else ref[first : first + rows, :]
        part = part.astype(jnp.float32)
        total = part if total is None else total + part
    out_ref[...] = total.astype(out_ref.dtype)


def add_rows(first, rows, out_type, *terms):
    return pl.pallas_call(
        functools.partial(add_kernel, first),
        out_shape=jax.ShapeDtypeStruct((rows, terms[0].shape[1]), out_type),
        in_specs=[VMEM] * len(terms),
        out_specs=VMEM,
        compiler_params=pltpu.CompilerParams(vmem_limit_bytes=8 << 20),
    )(*terms)


def shards(tokens, expert_ids, gate_weights, w_gate, w_up, w_down):
    tok_rows, model_width = tokens.shape
    groups = lax.axis_size("grp")
    owners = lax.axis_size("exp")
    experts = groups * owners
    chips = owners // CORES
    mine = lax.axis_index("grp") * owners + lax.axis_index("exp")

    def along_grp(value, step, back=False):
        return move(value, "grp", [(i, partner(i, step, groups)) for i in range(groups)], back)

    def along_chip(value, step, back=False):
        pairs = [
            (i * CORES + c, partner(i, step, chips) * CORES + c)
            for i in range(chips)
            for c in range(CORES)
        ]
        return move(value, "exp", pairs, back)

    def along_core(value):
        return move(value, "exp", [(i, i ^ 1) for i in range(owners)], False)

    own = prepare(tokens, expert_ids, gate_weights, experts)
    same, *weights = load_weights(own, w_gate, w_up, w_down)
    apply = functools.partial(expert_rows, mine[None], model_width, weights)
    width = groups if experts * tok_rows <= WHOLE_ROWS else 1
    total = None
    for first in range(0, groups, width):
        if first:
            own, total = lax.optimization_barrier((own, total))
        steps = range(first, first + width)
        line = [along_grp(own, g) if g else own for g in steps]
        ahead = [piece if first + at else same for at, piece in enumerate(line)]
        far = [along_chip(piece, s) for piece in ahead for s in range(1, chips)]
        near = jnp.concatenate(line, axis=0)
        near_back = along_core(apply(along_core(near), jnp.bfloat16))
        near_kept = apply(near, jnp.float32)
        far = jnp.concatenate(far, axis=0)
        far_back = along_core(apply(along_core(far), jnp.bfloat16))
        far_kept = apply(far, jnp.float32)
        for at, g in reversed(list(enumerate(steps))):
            terms = []
            for s in range(1, chips):
                start = (at * (chips - 1) + s - 1) * tok_rows
                piece = add_rows(start, tok_rows, jnp.bfloat16, far_kept, far_back)
                terms.append(along_chip(piece, s, True))
            begin = at * tok_rows
            if g:
                piece = add_rows(begin, tok_rows, jnp.bfloat16, near_kept, near_back, *terms)
                piece = along_grp(piece, g, True).astype(jnp.float32)
            else:
                piece = near_kept[begin : begin + tok_rows]
                for term in [near_back[begin : begin + tok_rows]] + terms:
                    piece = piece + term.astype(jnp.float32)
            total = piece if total is None else total + piece
    return total


def solution(mesh):
    return jax.shard_map(
        shards,
        mesh=mesh,
        in_specs=(
            P(("rep", "grp", "exp"), None),
            P(("rep", "grp", "exp"), None),
            P(("rep", "grp", "exp"), None),
            P(("grp", "exp"), None, None),
            P(("grp", "exp"), None, None),
            P(("grp", "exp"), None, None),
        ),
        out_specs=P(("rep", "grp", "exp"), None),
        check_vma=False,
    )
```

```python
import functools

import jax
import jax.numpy as jnp
from jax import lax
from jax.experimental import pallas as pl
from jax.experimental.pallas import tpu as pltpu
from jax.sharding import PartitionSpec as P

CORES = 2
LANES = 128
WHOLE_ROWS = 512
VMEM = pl.BlockSpec(memory_space=pltpu.VMEM)
SMEM = pl.BlockSpec(memory_space=pltpu.SMEM)
HBM = pl.BlockSpec(memory_space=pltpu.HBM)


def partner(index, step, count):
    return index ^ step if count & (count - 1) == 0 else (index + step) % count


def move(value, axis, pairs, back):
    return lax.ppermute(value, axis, [(d, s) for s, d in pairs] if back else pairs)


def prep_kernel(ids_ref, gates_ref, tokens_ref, out_ref, ids_held, gates_held, sems):
    model_width = tokens_ref.shape[1]
    copies = [
        pltpu.make_async_copy(ids_ref, ids_held, sems.at[0]),
        pltpu.make_async_copy(gates_ref, gates_held, sems.at[1]),
        pltpu.make_async_copy(tokens_ref, out_ref.at[:, :model_width], sems.at[2]),
    ]
    for copy in copies:
        copy.start()
    copies[0].wait()
    copies[1].wait()
    width = out_ref.shape[1] - model_width
    top_count, rows = ids_held.shape
    ids = ids_held[...]
    gates = gates_held[...].astype(jnp.float32)
    expert = lax.broadcasted_iota(jnp.int32, (width, rows), 0)
    turned = jnp.zeros((width, rows), jnp.float32)
    for k in range(top_count):
        turned += jnp.where(ids[k : k + 1, :] == expert, gates[k : k + 1, :], 0.0)
    same = lax.broadcasted_iota(jnp.int32, (rows, rows), 0) == lax.broadcasted_iota(
        jnp.int32, (rows, rows), 1
    )
    table = lax.dot_general(
        same.astype(jnp.bfloat16),
        turned.astype(jnp.bfloat16),
        (((1,), (1,)), ((), ())),
        preferred_element_type=jnp.float32,
    )
    out_ref[:, model_width:] = table.astype(jnp.bfloat16)
    copies[2].wait()


def prepare(tokens, expert_ids, gate_weights, experts):
    rows, model_width = tokens.shape
    top_count = expert_ids.shape[1]
    width = experts + -experts % LANES
    return pl.pallas_call(
        prep_kernel,
        out_shape=jax.ShapeDtypeStruct((rows, model_width + width), jnp.bfloat16),
        in_specs=[HBM] * 3,
        out_specs=VMEM,
        scratch_shapes=[
            pltpu.VMEM((top_count, rows), jnp.int32),
            pltpu.VMEM((top_count, rows), jnp.bfloat16),
            pltpu.SemaphoreType.DMA((3,)),
        ],
        compiler_params=pltpu.CompilerParams(vmem_limit_bytes=8 << 20),
    )(expert_ids.T, gate_weights.T, tokens)


def load_kernel(parts, *refs):
    sems = refs[-1]
    count = (len(refs) - 2) // 2
    done_ref = refs[2 * count]
    copies = []
    for at in range(count):
        source, target = refs[at].at[0], refs[count + at]
        rows = target.shape[0] // parts
        for part in range(parts):
            piece = pl.ds(part * rows, rows)
            copies.append(
                pltpu.make_async_copy(source.at[piece], target.at[piece], sems.at[at * parts + part])
            )
    for copy in copies:
        copy.start()
    done_ref[...] = jnp.zeros_like(done_ref)
    for copy in copies:
        copy.wait()


def load_weights(*weights):
    parts = 4
    out = [jax.ShapeDtypeStruct(w.shape[1:], w.dtype) for w in weights]
    out.append(jax.ShapeDtypeStruct((8, LANES), jnp.float32))
    return pl.pallas_call(
        functools.partial(load_kernel, parts),
        out_shape=out,
        in_specs=[HBM] * len(weights),
        out_specs=[VMEM] * len(out),
        scratch_shapes=[pltpu.SemaphoreType.DMA((parts * len(weights),))],
        compiler_params=pltpu.CompilerParams(vmem_limit_bytes=43 << 20),
        cost_estimate=pl.CostEstimate(
            flops=0, bytes_accessed=sum(w.size for w in weights) * 2, transcendentals=0
        ),
    )(*weights)


def expert_kernel(rows, mine_ref, x_ref, gate_ref, up_ref, down_ref, *refs):
    out_ref = refs[-1]
    model_width = out_ref.shape[1]

    def body(step, carry):
        part = pl.ds(pl.multiple_of(step * rows, rows), rows)
        x = x_ref[part, :model_width]
        table = x_ref[part, model_width:].astype(jnp.float32)
        lane = lax.broadcasted_iota(jnp.int32, table.shape, 1)
        scale = jnp.sum(jnp.where(lane == mine_ref[0], table, 0.0), axis=1, keepdims=True)
        gate_pre = jnp.dot(x, gate_ref[...], preferred_element_type=jnp.float32)
        up_pre = jnp.dot(x, up_ref[...], preferred_element_type=jnp.float32)
        hidden = (gate_pre / (1.0 + jnp.exp(-gate_pre)) * up_pre).astype(jnp.bfloat16)
        result = jnp.dot(hidden, down_ref[...], preferred_element_type=jnp.float32)
        out_ref[part, :] = (result * scale).astype(out_ref.dtype)
        return carry

    lax.fori_loop(0, x_ref.shape[0] // rows, body, 0)


def expert_rows(mine, model_width, weights, x, out_type, *after):
    total = x.shape[0]
    rows = next(r for r in range(min(total, 256), 0, -1) if total % r == 0)
    hidden_width = weights[0].shape[1]
    return pl.pallas_call(
        functools.partial(expert_kernel, rows),
        out_shape=jax.ShapeDtypeStruct((total, model_width), out_type),
        in_specs=[SMEM] + [VMEM] * 4 + [HBM] * len(after),
        out_specs=VMEM,
        compiler_params=pltpu.CompilerParams(vmem_limit_bytes=16 << 20),
        cost_estimate=pl.CostEstimate(
            flops=6 * total * model_width * hidden_width,
            bytes_accessed=0,
            transcendentals=total * hidden_width,
        ),
    )(mine, x, *weights, *after)


def pack_kernel(count, *refs):
    out_ref, at = refs[-1], 0
    for ref in refs[:count]:
        out_ref[at : at + ref.shape[0], :] = ref[...]
        at += ref.shape[0]


def pack(pieces, *after):
    rows = sum(piece.shape[0] for piece in pieces)
    return pl.pallas_call(
        functools.partial(pack_kernel, len(pieces)),
        out_shape=jax.ShapeDtypeStruct((rows, pieces[0].shape[1]), pieces[0].dtype),
        in_specs=[VMEM] * len(pieces) + [HBM] * len(after),
        out_specs=VMEM,
        compiler_params=pltpu.CompilerParams(vmem_limit_bytes=8 << 20),
    )(*pieces, *after)


def add_kernel(first, *refs):
    out_ref = refs[-1]
    rows = out_ref.shape[0]
    total = None
    for ref in refs[:-1]:
        part = ref[...] if ref.shape[0] == rows else ref[first : first + rows, :]
        part = part.astype(jnp.float32)
        total = part if total is None else total + part
    out_ref[...] = total.astype(out_ref.dtype)


def add_rows(first, rows, out_type, *terms):
    return pl.pallas_call(
        functools.partial(add_kernel, first),
        out_shape=jax.ShapeDtypeStruct((rows, terms[0].shape[1]), out_type),
        in_specs=[VMEM] * len(terms),
        out_specs=VMEM,
        compiler_params=pltpu.CompilerParams(vmem_limit_bytes=8 << 20),
    )(*terms)


def shards(tokens, expert_ids, gate_weights, w_gate, w_up, w_down):
    tok_rows, model_width = tokens.shape
    groups = lax.axis_size("grp")
    owners = lax.axis_size("exp")
    experts = groups * owners
    chips = owners // CORES
    mine = lax.axis_index("grp") * owners + lax.axis_index("exp")

    def along_grp(value, step, back=False):
        return move(value, "grp", [(i, partner(i, step, groups)) for i in range(groups)], back)

    def along_chip(value, step, back=False):
        pairs = [
            (i * CORES + c, partner(i, step, chips) * CORES + c)
            for i in range(chips)
            for c in range(CORES)
        ]
        return move(value, "exp", pairs, back)

    def along_core(value):
        return move(value, "exp", [(i, i ^ 1) for i in range(owners)], False)

    own = prepare(tokens, expert_ids, gate_weights, experts)
    *weights, loaded = load_weights(w_gate, w_up, w_down)
    apply = functools.partial(expert_rows, mine[None], model_width, weights)
    width = groups if experts * tok_rows <= WHOLE_ROWS else 1
    total = None
    for first in range(0, groups, width):
        if first:
            own, total = lax.optimization_barrier((own, total))
        steps = range(first, first + width)
        line = [along_grp(own, g) if g else own for g in steps]
        far = [along_chip(piece, s) for piece in line for s in range(1, chips)]
        near = pack(line)
        near_other = along_core(near)
        far = pack(far, loaded)
        far_other = along_core(far)
        near_kept = apply(near, jnp.float32)
        far_back = along_core(apply(far_other, jnp.bfloat16, near_kept))
        near_back = along_core(apply(near_other, jnp.bfloat16))
        far_kept = apply(far, jnp.float32)
        for at, g in reversed(list(enumerate(steps))):
            terms = []
            for s in range(1, chips):
                start = (at * (chips - 1) + s - 1) * tok_rows
                piece = add_rows(start, tok_rows, jnp.bfloat16, far_kept, far_back)
                terms.append(along_chip(piece, s, True))
            begin = at * tok_rows
            if g:
                piece = add_rows(begin, tok_rows, jnp.bfloat16, near_kept, near_back, *terms)
                piece = along_grp(piece, g, True).astype(jnp.float32)
            else:
                piece = near_kept[begin : begin + tok_rows]
                for term in [near_back[begin : begin + tok_rows]] + terms:
                    piece = piece + term.astype(jnp.float32)
            total = piece if total is None else total + piece
    return total


def solution(mesh):
    return jax.shard_map(
        shards,
        mesh=mesh,
        in_specs=(
            P(("rep", "grp", "exp"), None),
            P(("rep", "grp", "exp"), None),
            P(("rep", "grp", "exp"), None),
            P(("grp", "exp"), None, None),
            P(("grp", "exp"), None, None),
            P(("grp", "exp"), None, None),
        ),
        out_specs=P(("rep", "grp", "exp"), None),
        check_vma=False,
    )
```

```python
import functools

import jax
import jax.numpy as jnp
from jax import lax
from jax.experimental import pallas as pl
from jax.experimental.pallas import tpu as pltpu
from jax.sharding import PartitionSpec as P

CORES = 2
LANES = 128
WHOLE_ROWS = 512
LOAD_MIB = 43
VMEM = pl.BlockSpec(memory_space=pltpu.VMEM)
SMEM = pl.BlockSpec(memory_space=pltpu.SMEM)
HBM = pl.BlockSpec(memory_space=pltpu.HBM)


def partner(index, step, count):
    return index ^ step if count & (count - 1) == 0 else (index + step) % count


def move(value, axis, pairs, back):
    return lax.ppermute(value, axis, [(d, s) for s, d in pairs] if back else pairs)


def prep_kernel(mine_ref, ids_ref, gates_ref, tokens_ref, out_ref, place_ref, ids_held, gates_held, sems):
    model_width = tokens_ref.shape[1]
    copies = [
        pltpu.make_async_copy(ids_ref, ids_held, sems.at[0]),
        pltpu.make_async_copy(gates_ref, gates_held, sems.at[1]),
        pltpu.make_async_copy(tokens_ref, out_ref.at[:, :model_width], sems.at[2]),
    ]
    for copy in copies:
        copy.start()
    place_ref[...] = jnp.zeros_like(place_ref) + mine_ref[0]
    copies[0].wait()
    copies[1].wait()
    width = out_ref.shape[1] - model_width
    top_count, rows = ids_held.shape
    ids = ids_held[...]
    gates = gates_held[...].astype(jnp.float32)
    expert = lax.broadcasted_iota(jnp.int32, (width, rows), 0)
    turned = jnp.zeros((width, rows), jnp.float32)
    for k in range(top_count):
        turned += jnp.where(ids[k : k + 1, :] == expert, gates[k : k + 1, :], 0.0)
    same = lax.broadcasted_iota(jnp.int32, (rows, rows), 0) == lax.broadcasted_iota(
        jnp.int32, (rows, rows), 1
    )
    table = lax.dot_general(
        same.astype(jnp.bfloat16),
        turned.astype(jnp.bfloat16),
        (((1,), (1,)), ((), ())),
        preferred_element_type=jnp.float32,
    )
    out_ref[:, model_width:] = table.astype(jnp.bfloat16)
    copies[2].wait()


def prepare(mine, tokens, expert_ids, gate_weights, experts):
    rows, model_width = tokens.shape
    top_count = expert_ids.shape[1]
    width = experts + -experts % LANES
    return pl.pallas_call(
        prep_kernel,
        out_shape=[
            jax.ShapeDtypeStruct((rows, model_width + width), jnp.bfloat16),
            jax.ShapeDtypeStruct((8, width), jnp.int32),
        ],
        in_specs=[SMEM] + [HBM] * 3,
        out_specs=[VMEM] * 2,
        scratch_shapes=[
            pltpu.VMEM((top_count, rows), jnp.int32),
            pltpu.VMEM((top_count, rows), jnp.bfloat16),
            pltpu.SemaphoreType.DMA((3,)),
        ],
        compiler_params=pltpu.CompilerParams(vmem_limit_bytes=8 << 20),
    )(mine, expert_ids.T, gate_weights.T, tokens)


def row_scale(place_ref, table):
    table = table.astype(jnp.float32)
    lane = lax.broadcasted_iota(jnp.int32, table.shape, 1)
    return jnp.sum(jnp.where(lane == place_ref[:1, :], table, 0.0), axis=1, keepdims=True)


def activate(gate_pre, up_pre):
    return (gate_pre / (1.0 + jnp.exp(-gate_pre)) * up_pre).astype(jnp.bfloat16)


def load_kernel(parts, *refs):
    sems = refs[-1]
    count = (len(refs) - 2) // 2
    done_ref = refs[2 * count]
    copies = []
    for at in range(count):
        source, target = refs[at].at[0], refs[count + at]
        rows = target.shape[0] // parts
        for part in range(parts):
            piece = pl.ds(part * rows, rows)
            copies.append(
                pltpu.make_async_copy(source.at[piece], target.at[piece], sems.at[at * parts + part])
            )
    for copy in copies:
        copy.start()
    done_ref[...] = jnp.zeros_like(done_ref)
    for copy in copies:
        copy.wait()


def load_weights(*weights):
    parts = 4
    out = [jax.ShapeDtypeStruct(w.shape[1:], w.dtype) for w in weights]
    out.append(jax.ShapeDtypeStruct((8, LANES), jnp.float32))
    return pl.pallas_call(
        functools.partial(load_kernel, parts),
        out_shape=out,
        in_specs=[HBM] * len(weights),
        out_specs=[VMEM] * len(out),
        scratch_shapes=[pltpu.SemaphoreType.DMA((parts * len(weights),))],
        compiler_params=pltpu.CompilerParams(vmem_limit_bytes=LOAD_MIB << 20),
        cost_estimate=pl.CostEstimate(
            flops=0, bytes_accessed=sum(w.size for w in weights) * 2, transcendentals=0
        ),
    )(*weights)


def expert_kernel(rows, count, place_ref, *refs):
    inputs, outputs, held = refs[:count], refs[-count - 1 : -1], refs[-1]
    gate_ref, up_ref, down_ref = refs[count : count + 3]
    model_width = outputs[0].shape[1]

    def body(step, carry):
        part = pl.ds(pl.multiple_of(step * rows, rows), rows)
        for at, ref in enumerate(inputs):
            held[at * rows : (at + 1) * rows] = ref[part, :]
        x = held[:, :model_width]
        scale = row_scale(place_ref, held[:, model_width:])
        gate_pre = jnp.dot(x, gate_ref[...], preferred_element_type=jnp.float32)
        up_pre = jnp.dot(x, up_ref[...], preferred_element_type=jnp.float32)
        hidden = activate(gate_pre, up_pre)
        result = jnp.dot(hidden, down_ref[...], preferred_element_type=jnp.float32) * scale
        for at, ref in enumerate(outputs):
            ref[part, :] = result[at * rows : (at + 1) * rows].astype(ref.dtype)
        return carry

    lax.fori_loop(0, inputs[0].shape[0] // rows, body, 0)


def expert_rows(place, weights, blocks, types, *after):
    total, width = blocks[0].shape
    model_width, hidden_width = weights[0].shape
    count = len(blocks)
    rows = next(r for r in range(min(total, 128), 0, -1) if total % r == 0 and r % 16 == 0)
    return pl.pallas_call(
        functools.partial(expert_kernel, rows, count),
        out_shape=[jax.ShapeDtypeStruct((total, model_width), kind) for kind in types],
        in_specs=[VMEM] * (count + 4) + [HBM] * len(after),
        out_specs=[VMEM] * count,
        scratch_shapes=[pltpu.VMEM((count * rows, width), jnp.bfloat16)],
        compiler_params=pltpu.CompilerParams(vmem_limit_bytes=16 << 20),
        cost_estimate=pl.CostEstimate(
            flops=6 * count * total * model_width * hidden_width,
            bytes_accessed=0,
            transcendentals=count * total * hidden_width,
        ),
    )(place, *blocks, *weights, *after)


def pack_kernel(count, *refs):
    out_ref, at = refs[-1], 0
    for ref in refs[:count]:
        out_ref[at : at + ref.shape[0], :] = ref[...]
        at += ref.shape[0]


def pack(pieces, *after):
    rows = sum(piece.shape[0] for piece in pieces)
    return pl.pallas_call(
        functools.partial(pack_kernel, len(pieces)),
        out_shape=jax.ShapeDtypeStruct((rows, pieces[0].shape[1]), pieces[0].dtype),
        in_specs=[VMEM] * len(pieces) + [HBM] * len(after),
        out_specs=VMEM,
        compiler_params=pltpu.CompilerParams(vmem_limit_bytes=8 << 20),
    )(*pieces, *after)


def add_kernel(first, *refs):
    out_ref = refs[-1]
    rows = out_ref.shape[0]
    total = None
    for ref in refs[:-1]:
        part = ref[...] if ref.shape[0] == rows else ref[first : first + rows, :]
        part = part.astype(jnp.float32)
        total = part if total is None else total + part
    out_ref[...] = total.astype(out_ref.dtype)


def add_rows(first, rows, out_type, *terms):
    return pl.pallas_call(
        functools.partial(add_kernel, first),
        out_shape=jax.ShapeDtypeStruct((rows, terms[0].shape[1]), out_type),
        in_specs=[VMEM] * len(terms),
        out_specs=VMEM,
        compiler_params=pltpu.CompilerParams(vmem_limit_bytes=8 << 20),
    )(*terms)


def shards(tokens, expert_ids, gate_weights, w_gate, w_up, w_down):
    tok_rows, model_width = tokens.shape
    groups = lax.axis_size("grp")
    owners = lax.axis_size("exp")
    experts = groups * owners
    chips = owners // CORES
    mine = lax.axis_index("grp") * owners + lax.axis_index("exp")

    def along_grp(value, step, back=False):
        return move(value, "grp", [(i, partner(i, step, groups)) for i in range(groups)], back)

    def along_chip(value, step, back=False):
        pairs = [
            (i * CORES + c, partner(i, step, chips) * CORES + c)
            for i in range(chips)
            for c in range(CORES)
        ]
        return move(value, "exp", pairs, back)

    def along_core(value):
        return move(value, "exp", [(i, i ^ 1) for i in range(owners)], False)

    own, place = prepare(mine[None], tokens, expert_ids, gate_weights, experts)
    *weights, loaded = load_weights(w_gate, w_up, w_down)
    width = groups if experts * tok_rows <= WHOLE_ROWS else 1
    total = None
    for first in range(0, groups, width):
        if first:
            own, total = lax.optimization_barrier((own, total))
        steps = range(first, first + width)
        line = [along_grp(own, g) if g else own for g in steps]
        far = [along_chip(piece, s) for piece in line for s in range(1, chips)]
        far = pack(far, loaded)
        far_other = along_core(far)
        near = pack(line, far_other)
        near_other = along_core(near)
        types = (jnp.float32, jnp.bfloat16)
        far_kept, far_back = expert_rows(place, weights, [far, far_other], types)
        near_kept, near_back = expert_rows(place, weights, [near, near_other], types, far_kept)
        far_back, near_back = along_core(far_back), along_core(near_back)
        for at, g in reversed(list(enumerate(steps))):
            terms = []
            for s in range(1, chips):
                start = (at * (chips - 1) + s - 1) * tok_rows
                piece = add_rows(start, tok_rows, jnp.bfloat16, far_kept, far_back)
                terms.append(along_chip(piece, s, True))
            begin = at * tok_rows
            if g:
                piece = add_rows(begin, tok_rows, jnp.bfloat16, near_kept, near_back, *terms)
                piece = along_grp(piece, g, True).astype(jnp.float32)
            else:
                piece = near_kept[begin : begin + tok_rows]
                for term in [near_back[begin : begin + tok_rows]] + terms:
                    piece = piece + term.astype(jnp.float32)
            total = piece if total is None else total + piece
    return total


def solution(mesh):
    return jax.shard_map(
        shards,
        mesh=mesh,
        in_specs=(
            P(("rep", "grp", "exp"), None),
            P(("rep", "grp", "exp"), None),
            P(("rep", "grp", "exp"), None),
            P(("grp", "exp"), None, None),
            P(("grp", "exp"), None, None),
            P(("grp", "exp"), None, None),
        ),
        out_specs=P(("rep", "grp", "exp"), None),
        check_vma=False,
    )
```

```python
import functools

import jax
import jax.numpy as jnp
from jax import lax
from jax.experimental import pallas as pl
from jax.experimental.pallas import tpu as pltpu
from jax.sharding import PartitionSpec as P

CORES = 2
LANES = 128
WHOLE_ROWS = 512
PLACE_FLOPS = 1 << 31
PREP_FLOPS = 1 << 35
VMEM = pl.BlockSpec(memory_space=pltpu.VMEM)
SMEM = pl.BlockSpec(memory_space=pltpu.SMEM)
HBM = pl.BlockSpec(memory_space=pltpu.HBM)


def partner(index, step, count):
    return index ^ step if count & (count - 1) == 0 else (index + step) % count


def place_kernel(mine_ref, out_ref):
    out_ref[...] = jnp.zeros_like(out_ref) + mine_ref[0]


def find_place(mine, width):
    return pl.pallas_call(
        place_kernel,
        out_shape=jax.ShapeDtypeStruct((8, width), jnp.int32),
        in_specs=[SMEM],
        out_specs=VMEM,
        compiler_params=pltpu.CompilerParams(vmem_limit_bytes=8 << 20),
        cost_estimate=pl.CostEstimate(flops=PLACE_FLOPS, bytes_accessed=0, transcendentals=0),
    )(mine)


def prep_kernel(place_ref, ids_ref, gates_ref, tokens_ref, out_ref):
    model_width = tokens_ref.shape[1]
    width = out_ref.shape[1] - model_width
    out_ref[:, :model_width] = tokens_ref[...]
    ids = ids_ref[...]
    gates = gates_ref[...].astype(jnp.float32)
    top_count, rows = ids.shape
    expert = lax.broadcasted_iota(jnp.int32, (width, rows), 0)
    turned = jnp.zeros((width, rows), jnp.float32)
    for k in range(top_count):
        turned += jnp.where(ids[k : k + 1, :] == expert, gates[k : k + 1, :], 0.0)
    same = lax.broadcasted_iota(jnp.int32, (rows, rows), 0) == lax.broadcasted_iota(
        jnp.int32, (rows, rows), 1
    )
    table = lax.dot_general(
        same.astype(jnp.bfloat16),
        turned.astype(jnp.bfloat16),
        (((1,), (1,)), ((), ())),
        preferred_element_type=jnp.float32,
    )
    out_ref[:, model_width:] = table.astype(jnp.bfloat16)


def prepare(place, tokens, expert_ids, gate_weights):
    rows, model_width = tokens.shape
    return pl.pallas_call(
        prep_kernel,
        out_shape=jax.ShapeDtypeStruct((rows, model_width + place.shape[1]), jnp.bfloat16),
        in_specs=[HBM] + [VMEM] * 3,
        out_specs=VMEM,
        compiler_params=pltpu.CompilerParams(vmem_limit_bytes=8 << 20),
        cost_estimate=pl.CostEstimate(flops=PREP_FLOPS, bytes_accessed=0, transcendentals=0),
    )(place, expert_ids.T, gate_weights.T, tokens)


def row_scale(place_ref, table):
    table = table.astype(jnp.float32)
    lane = lax.broadcasted_iota(jnp.int32, table.shape, 1)
    return jnp.sum(jnp.where(lane == place_ref[:1, :], table, 0.0), axis=1, keepdims=True)


def activate(gate_pre, up_pre):
    return (gate_pre / (1.0 + jnp.exp(-gate_pre)) * up_pre).astype(jnp.bfloat16)


def expert_kernel(count, place_ref, *refs):
    kept_ref, given_ref, held = refs[-3:]
    gate_ref, up_ref, down_ref = refs[count : count + 3]
    rows, model_width = kept_ref.shape
    each = refs[0].shape[0]
    for at, ref in enumerate(refs[:count]):
        held[at * each : (at + 1) * each] = ref[...]
    x = held[:, :model_width]
    scale = row_scale(place_ref, held[:, model_width:])
    gate_pre = jnp.dot(x, gate_ref[0], preferred_element_type=jnp.float32)
    up_pre = jnp.dot(x, up_ref[0], preferred_element_type=jnp.float32)
    hidden = activate(gate_pre, up_pre)
    result = jnp.dot(hidden, down_ref[0], preferred_element_type=jnp.float32) * scale
    kept_ref[...] = result[:rows]
    given_ref[...] = result[rows:].astype(given_ref.dtype)


def expert_rows(place, weights, own, other, *after):
    each, width = own[0].shape
    _, model_width, hidden_width = weights[0].shape
    count = 2 * len(own)
    rows = len(own) * each
    return pl.pallas_call(
        functools.partial(expert_kernel, count),
        out_shape=[
            jax.ShapeDtypeStruct((rows, model_width), jnp.float32),
            jax.ShapeDtypeStruct((rows, model_width), jnp.bfloat16),
        ],
        in_specs=[VMEM] * (count + 4) + [HBM] * len(after),
        out_specs=[VMEM] * 2,
        scratch_shapes=[pltpu.VMEM((count * each, width), jnp.bfloat16)],
        compiler_params=pltpu.CompilerParams(vmem_limit_bytes=16 << 20),
        cost_estimate=pl.CostEstimate(
            flops=12 * rows * model_width * hidden_width,
            bytes_accessed=0,
            transcendentals=2 * rows * hidden_width,
        ),
    )(place, *own, *other, *weights, *after)


def later_kernel(source_ref, after_ref, out_ref):
    out_ref[...] = source_ref[...]


def later(piece, after):
    return pl.pallas_call(
        later_kernel,
        out_shape=jax.ShapeDtypeStruct(piece.shape, piece.dtype),
        in_specs=[VMEM, HBM],
        out_specs=VMEM,
        compiler_params=pltpu.CompilerParams(vmem_limit_bytes=8 << 20),
    )(piece, after)


def add_kernel(first, *refs):
    out_ref = refs[-1]
    rows = out_ref.shape[0]
    total = None
    for ref in refs[:-1]:
        part = ref[...] if ref.shape[0] == rows else ref[first : first + rows, :]
        part = part.astype(jnp.float32)
        total = part if total is None else total + part
    out_ref[...] = total.astype(out_ref.dtype)


def add_rows(first, rows, out_type, *terms):
    return pl.pallas_call(
        functools.partial(add_kernel, first),
        out_shape=jax.ShapeDtypeStruct((rows, terms[0].shape[1]), out_type),
        in_specs=[VMEM] * len(terms),
        out_specs=VMEM,
        compiler_params=pltpu.CompilerParams(vmem_limit_bytes=8 << 20),
    )(*terms)


def shards(tokens, expert_ids, gate_weights, w_gate, w_up, w_down):
    tok_rows, model_width = tokens.shape
    groups = lax.axis_size("grp")
    owners = lax.axis_size("exp")
    experts = groups * owners
    chips = owners // CORES
    mine = lax.axis_index("grp") * owners + lax.axis_index("exp")

    def step_to(value, g, s, back=False):
        pairs = [
            (
                (i * chips + j) * CORES + c,
                (partner(i, g, groups) * chips + partner(j, s, chips)) * CORES + c,
            )
            for i in range(groups)
            for j in range(chips)
            for c in range(CORES)
        ]
        return lax.ppermute(value, ("grp", "exp"), [(d, o) for o, d in pairs] if back else pairs)

    def swap(value):
        return lax.ppermute(value, "exp", [(i, i ^ 1) for i in range(owners)])

    place = find_place(mine[None], experts + -experts % LANES)
    own = prepare(place, tokens, expert_ids, gate_weights)
    weights = (w_gate, w_up, w_down)
    width = groups if experts * tok_rows <= WHOLE_ROWS else 1
    total = None
    for first in range(0, groups, width):
        if first:
            own, total = lax.optimization_barrier((own, total))
        steps = range(first, first + width)
        near = [step_to(own, g, 0) if g else own for g in steps]
        far = [step_to(piece, 0, s) for piece in near for s in range(1, chips)]
        near_kept, near_back = expert_rows(place, weights, near, [swap(piece) for piece in near])
        near_back = swap(near_back)
        late = min(1, width - 1) * (chips - 1)
        given = [later(piece, near_kept) if at == late else piece for at, piece in enumerate(far)]
        far_kept, far_back = expert_rows(
            place, weights, far, [swap(piece) for piece in given], near_kept
        )
        far_back = swap(far_back)
        terms = []
        for at, g in reversed(list(enumerate(steps))):
            begin = at * tok_rows
            if g:
                piece = add_rows(begin, tok_rows, jnp.bfloat16, near_kept, near_back)
                terms.append(step_to(piece, g, 0, True))
            else:
                terms += [part[begin : begin + tok_rows] for part in (near_kept, near_back)]
        for at, g in reversed(list(enumerate(steps))):
            for s in range(1, chips):
                begin = (at * (chips - 1) + s - 1) * tok_rows
                piece = add_rows(begin, tok_rows, jnp.bfloat16, far_kept, far_back)
                terms.append(step_to(piece, g, s, True))
        for term in terms:
            term = term.astype(jnp.float32)
            total = term if total is None else total + term
    return total


def solution(mesh):
    return jax.shard_map(
        shards,
        mesh=mesh,
        in_specs=(
            P(("rep", "grp", "exp"), None),
            P(("rep", "grp", "exp"), None),
            P(("rep", "grp", "exp"), None),
            P(("grp", "exp"), None, None),
            P(("grp", "exp"), None, None),
            P(("grp", "exp"), None, None),
        ),
        out_specs=P(("rep", "grp", "exp"), None),
        check_vma=False,
    )
```

```python
import functools

import jax
import jax.numpy as jnp
from jax import lax
from jax.experimental import pallas as pl
from jax.experimental.pallas import tpu as pltpu
from jax.sharding import PartitionSpec as P

CORES = 2
LANES = 128
WHOLE_ROWS = 512
PLACE_FLOPS = 1 << 31
PREP_FLOPS = 1 << 35
VMEM = pl.BlockSpec(memory_space=pltpu.VMEM)
SMEM = pl.BlockSpec(memory_space=pltpu.SMEM)
HBM = pl.BlockSpec(memory_space=pltpu.HBM)


def partner(index, step, count):
    return index ^ step if count & (count - 1) == 0 else (index + step) % count


def place_kernel(mine_ref, out_ref):
    out_ref[...] = jnp.zeros_like(out_ref) + mine_ref[0]


def find_place(mine, width):
    return pl.pallas_call(
        place_kernel,
        out_shape=jax.ShapeDtypeStruct((8, width), jnp.int32),
        in_specs=[SMEM],
        out_specs=VMEM,
        compiler_params=pltpu.CompilerParams(vmem_limit_bytes=8 << 20),
        cost_estimate=pl.CostEstimate(flops=PLACE_FLOPS, bytes_accessed=0, transcendentals=0),
    )(mine)


def prep_kernel(place_ref, ids_ref, gates_ref, tokens_ref, out_ref):
    model_width = tokens_ref.shape[1]
    width = out_ref.shape[1] - model_width
    out_ref[:, :model_width] = tokens_ref[...]
    ids = ids_ref[...]
    gates = gates_ref[...].astype(jnp.float32)
    top_count, rows = ids.shape
    expert = lax.broadcasted_iota(jnp.int32, (width, rows), 0)
    turned = jnp.zeros((width, rows), jnp.float32)
    for k in range(top_count):
        turned += jnp.where(ids[k : k + 1, :] == expert, gates[k : k + 1, :], 0.0)
    same = lax.broadcasted_iota(jnp.int32, (rows, rows), 0) == lax.broadcasted_iota(
        jnp.int32, (rows, rows), 1
    )
    table = lax.dot_general(
        same.astype(jnp.bfloat16),
        turned.astype(jnp.bfloat16),
        (((1,), (1,)), ((), ())),
        preferred_element_type=jnp.float32,
    )
    out_ref[:, model_width:] = table.astype(jnp.bfloat16)


def prepare(place, tokens, expert_ids, gate_weights):
    rows, model_width = tokens.shape
    return pl.pallas_call(
        prep_kernel,
        out_shape=jax.ShapeDtypeStruct((rows, model_width + place.shape[1]), jnp.bfloat16),
        in_specs=[HBM] + [VMEM] * 3,
        out_specs=VMEM,
        compiler_params=pltpu.CompilerParams(vmem_limit_bytes=8 << 20),
        cost_estimate=pl.CostEstimate(flops=PREP_FLOPS, bytes_accessed=0, transcendentals=0),
    )(place, expert_ids.T, gate_weights.T, tokens)


def row_scale(place_ref, table):
    table = table.astype(jnp.float32)
    lane = lax.broadcasted_iota(jnp.int32, table.shape, 1)
    return jnp.sum(jnp.where(lane == place_ref[:1, :], table, 0.0), axis=1, keepdims=True)


def activate(gate_pre, up_pre):
    return (gate_pre / (1.0 + jnp.exp(-gate_pre)) * up_pre).astype(jnp.bfloat16)


def join(pieces, out_ref):
    at = 0
    for ref in pieces:
        out_ref[at : at + ref.shape[0], :] = ref[...]
        at += ref.shape[0]


def expert_kernel(count, place_ref, *refs):
    kept_ref, given_ref, held = refs[-3:]
    gate_ref, up_ref, down_ref = refs[count : count + 3]
    rows, model_width = kept_ref.shape
    join(refs[:count], held)
    x = held[:, :model_width]
    scale = row_scale(place_ref, held[:, model_width:])
    gate_pre = jnp.dot(x, gate_ref[0], preferred_element_type=jnp.float32)
    up_pre = jnp.dot(x, up_ref[0], preferred_element_type=jnp.float32)
    hidden = activate(gate_pre, up_pre)
    result = jnp.dot(hidden, down_ref[0], preferred_element_type=jnp.float32) * scale
    kept_ref[...] = result[:rows]
    given_ref[...] = result[rows:].astype(given_ref.dtype)


def expert_rows(place, weights, own, other, *after):
    width = own[0].shape[1]
    _, model_width, hidden_width = weights[0].shape
    count = len(own) + len(other)
    rows = sum(piece.shape[0] for piece in own)
    return pl.pallas_call(
        functools.partial(expert_kernel, count),
        out_shape=[
            jax.ShapeDtypeStruct((rows, model_width), jnp.float32),
            jax.ShapeDtypeStruct((rows, model_width), jnp.bfloat16),
        ],
        in_specs=[VMEM] * (count + 4) + [HBM] * len(after),
        out_specs=[VMEM] * 2,
        scratch_shapes=[pltpu.VMEM((2 * rows, width), jnp.bfloat16)],
        compiler_params=pltpu.CompilerParams(vmem_limit_bytes=16 << 20),
        cost_estimate=pl.CostEstimate(
            flops=12 * rows * model_width * hidden_width,
            bytes_accessed=0,
            transcendentals=2 * rows * hidden_width,
        ),
    )(place, *own, *other, *weights, *after)


def pack_kernel(count, *refs):
    join(refs[:count], refs[-1])


def pack(pieces, *after):
    rows = sum(piece.shape[0] for piece in pieces)
    return pl.pallas_call(
        functools.partial(pack_kernel, len(pieces)),
        out_shape=jax.ShapeDtypeStruct((rows, pieces[0].shape[1]), pieces[0].dtype),
        in_specs=[VMEM] * len(pieces) + [HBM] * len(after),
        out_specs=VMEM,
        compiler_params=pltpu.CompilerParams(vmem_limit_bytes=8 << 20),
    )(*pieces, *after)


def add_kernel(first, *refs):
    out_ref = refs[-1]
    rows = out_ref.shape[0]
    total = None
    for ref in refs[:-1]:
        part = ref[...] if ref.shape[0] == rows else ref[first : first + rows, :]
        part = part.astype(jnp.float32)
        total = part if total is None else total + part
    out_ref[...] = total.astype(out_ref.dtype)


def add_rows(first, rows, out_type, *terms):
    return pl.pallas_call(
        functools.partial(add_kernel, first),
        out_shape=jax.ShapeDtypeStruct((rows, terms[0].shape[1]), out_type),
        in_specs=[VMEM] * len(terms),
        out_specs=VMEM,
        compiler_params=pltpu.CompilerParams(vmem_limit_bytes=8 << 20),
    )(*terms)


def shards(tokens, expert_ids, gate_weights, w_gate, w_up, w_down):
    tok_rows, model_width = tokens.shape
    groups = lax.axis_size("grp")
    owners = lax.axis_size("exp")
    experts = groups * owners
    chips = owners // CORES
    mine = lax.axis_index("grp") * owners + lax.axis_index("exp")

    def step_to(value, g, s, back=False):
        pairs = [
            (
                (i * chips + j) * CORES + c,
                (partner(i, g, groups) * chips + partner(j, s, chips)) * CORES + c,
            )
            for i in range(groups)
            for j in range(chips)
            for c in range(CORES)
        ]
        return lax.ppermute(value, ("grp", "exp"), [(d, o) for o, d in pairs] if back else pairs)

    def swap(value):
        return lax.ppermute(value, "exp", [(i, i ^ 1) for i in range(owners)])

    place = find_place(mine[None], experts + -experts % LANES)
    own = prepare(place, tokens, expert_ids, gate_weights)
    weights = (w_gate, w_up, w_down)
    width = groups if experts * tok_rows <= WHOLE_ROWS else 1
    total = None
    for first in range(0, groups, width):
        if first:
            own, total = lax.optimization_barrier((own, total))
        steps = range(first, first + width)
        near = [step_to(own, g, 0) if g else own for g in steps]
        far = [step_to(piece, 0, s) for piece in near for s in range(1, chips)]
        near_other = [swap(piece) for piece in near]
        far_block = pack(far, *near_other)
        near_kept, near_back = expert_rows(
            place, weights, near, near_other, far_block
        )
        far_kept, far_back = expert_rows(place, weights, [far_block], [swap(far_block)], near_kept)
        far_back, near_back = swap(far_back), swap(near_back)

        def near_sum(at, *terms):
            begin = at * tok_rows
            return add_rows(begin, tok_rows, jnp.bfloat16, near_kept, near_back, *terms)

        def far_sum(at, s):
            begin = (at * (chips - 1) + s - 1) * tok_rows
            return add_rows(begin, tok_rows, jnp.bfloat16, far_kept, far_back)

        terms = []
        if first == 0:
            terms += [part[:tok_rows] for part in (near_kept, near_back)]
        by_chip = {
            at: [step_to(far_sum(at, s), 0, s, True) for s in range(1, chips)]
            for at in reversed(range(width))
        }
        for at, g in reversed(list(enumerate(steps))):
            terms += [step_to(near_sum(at, *by_chip[at]), g, 0, True)] if g else by_chip[at]
        for term in terms:
            term = term.astype(jnp.float32)
            total = term if total is None else total + term
    return total


def solution(mesh):
    return jax.shard_map(
        shards,
        mesh=mesh,
        in_specs=(
            P(("rep", "grp", "exp"), None),
            P(("rep", "grp", "exp"), None),
            P(("rep", "grp", "exp"), None),
            P(("grp", "exp"), None, None),
            P(("grp", "exp"), None, None),
            P(("grp", "exp"), None, None),
        ),
        out_specs=P(("rep", "grp", "exp"), None),
        check_vma=False,
    )
```

```python
import functools

import jax
import jax.numpy as jnp
from jax import lax
from jax.experimental import pallas as pl
from jax.experimental.pallas import tpu as pltpu
from jax.sharding import PartitionSpec as P

CORES = 2
LANES = 128
WHOLE_ROWS = 512
PLACE_FLOPS = 1 << 31
PREP_FLOPS = 1 << 35
VMEM = pl.BlockSpec(memory_space=pltpu.VMEM)
SMEM = pl.BlockSpec(memory_space=pltpu.SMEM)
HBM = pl.BlockSpec(memory_space=pltpu.HBM)


def partner(index, step, count):
    return index ^ step if count & (count - 1) == 0 else (index + step) % count


def place_kernel(mine_ref, out_ref):
    out_ref[...] = jnp.zeros_like(out_ref) + mine_ref[0]


def find_place(mine, width):
    return pl.pallas_call(
        place_kernel,
        out_shape=jax.ShapeDtypeStruct((8, width), jnp.int32),
        in_specs=[SMEM],
        out_specs=VMEM,
        compiler_params=pltpu.CompilerParams(vmem_limit_bytes=8 << 20),
        cost_estimate=pl.CostEstimate(flops=PLACE_FLOPS, bytes_accessed=0, transcendentals=0),
    )(mine)


def prep_kernel(place_ref, ids_ref, gates_ref, tokens_ref, out_ref):
    model_width = tokens_ref.shape[1]
    width = out_ref.shape[1] - model_width
    out_ref[:, :model_width] = tokens_ref[...]
    ids = ids_ref[...]
    gates = gates_ref[...].astype(jnp.float32)
    top_count, rows = ids.shape
    expert = lax.broadcasted_iota(jnp.int32, (width, rows), 0)
    turned = jnp.zeros((width, rows), jnp.float32)
    for k in range(top_count):
        turned += jnp.where(ids[k : k + 1, :] == expert, gates[k : k + 1, :], 0.0)
    same = lax.broadcasted_iota(jnp.int32, (rows, rows), 0) == lax.broadcasted_iota(
        jnp.int32, (rows, rows), 1
    )
    table = lax.dot_general(
        same.astype(jnp.bfloat16),
        turned.astype(jnp.bfloat16),
        (((1,), (1,)), ((), ())),
        preferred_element_type=jnp.float32,
    )
    out_ref[:, model_width:] = table.astype(jnp.bfloat16)


def prepare(place, tokens, expert_ids, gate_weights):
    rows, model_width = tokens.shape
    return pl.pallas_call(
        prep_kernel,
        out_shape=jax.ShapeDtypeStruct((rows, model_width + place.shape[1]), jnp.bfloat16),
        in_specs=[HBM] + [VMEM] * 3,
        out_specs=VMEM,
        compiler_params=pltpu.CompilerParams(vmem_limit_bytes=8 << 20),
        cost_estimate=pl.CostEstimate(flops=PREP_FLOPS, bytes_accessed=0, transcendentals=0),
    )(place, expert_ids.T, gate_weights.T, tokens)


def row_scale(place_ref, table):
    table = table.astype(jnp.float32)
    lane = lax.broadcasted_iota(jnp.int32, table.shape, 1)
    return jnp.sum(jnp.where(lane == place_ref[:1, :], table, 0.0), axis=1, keepdims=True)


def activate(gate_pre, up_pre):
    return (gate_pre / (1.0 + jnp.exp(-gate_pre)) * up_pre).astype(jnp.bfloat16)


def join(pieces, out_ref):
    at = 0
    for ref in pieces:
        out_ref[at : at + ref.shape[0], :] = ref[...]
        at += ref.shape[0]


def expert_kernel(skip, count, starts, *refs):
    place_ref, *refs = refs[skip:]
    kept_ref, *given_refs, held = refs[-2 - len(starts) :]
    gate_ref, up_ref, down_ref = refs[count : count + 3]
    rows, model_width = kept_ref.shape
    join(refs[:count], held)
    x = held[:, :model_width]
    scale = row_scale(place_ref, held[:, model_width:])
    gate_pre = jnp.dot(x, gate_ref[0], preferred_element_type=jnp.float32)
    up_pre = jnp.dot(x, up_ref[0], preferred_element_type=jnp.float32)
    hidden = activate(gate_pre, up_pre)
    result = jnp.dot(hidden, down_ref[0], preferred_element_type=jnp.float32) * scale
    kept_ref[...] = result[:rows]
    for ref, at in zip(given_refs, starts):
        ref[...] = result[rows + at : rows + at + ref.shape[0]].astype(ref.dtype)


def expert_rows(place, weights, own, other, *after, alone=None):
    width = own[0].shape[1]
    _, model_width, hidden_width = weights[0].shape
    count = len(own) + len(other)
    rows = sum(piece.shape[0] for piece in own)
    starts, parts = [0], [rows]
    if alone is not None:
        starts.append(alone * own[0].shape[0])
        parts.append(own[0].shape[0])
    return pl.pallas_call(
        functools.partial(expert_kernel, len(after), count, starts),
        out_shape=[
            jax.ShapeDtypeStruct((rows, model_width), jnp.float32),
            *[jax.ShapeDtypeStruct((part, model_width), jnp.bfloat16) for part in parts],
        ],
        in_specs=[HBM] * len(after) + [VMEM] * (count + 4),
        out_specs=[VMEM] * (1 + len(parts)),
        scratch_shapes=[pltpu.VMEM((2 * rows, width), jnp.bfloat16)],
        compiler_params=pltpu.CompilerParams(vmem_limit_bytes=16 << 20),
        cost_estimate=pl.CostEstimate(
            flops=12 * rows * model_width * hidden_width,
            bytes_accessed=0,
            transcendentals=2 * rows * hidden_width,
        ),
    )(*after, place, *own, *other, *weights)


def pack_kernel(count, *refs):
    join(refs[:count], refs[-1])


def pack(pieces, *after):
    rows = sum(piece.shape[0] for piece in pieces)
    return pl.pallas_call(
        functools.partial(pack_kernel, len(pieces)),
        out_shape=jax.ShapeDtypeStruct((rows, pieces[0].shape[1]), pieces[0].dtype),
        in_specs=[VMEM] * len(pieces) + [HBM] * len(after),
        out_specs=VMEM,
        compiler_params=pltpu.CompilerParams(vmem_limit_bytes=8 << 20),
    )(*pieces, *after)


def add_kernel(first, count, *refs):
    out_ref = refs[-1]
    rows = out_ref.shape[0]
    total = None
    for ref in refs[:count]:
        part = ref[...] if ref.shape[0] == rows else ref[first : first + rows, :]
        part = part.astype(jnp.float32)
        total = part if total is None else total + part
    out_ref[...] = total.astype(out_ref.dtype)


def add_rows(first, rows, out_type, *terms, after=()):
    return pl.pallas_call(
        functools.partial(add_kernel, first, len(terms)),
        out_shape=jax.ShapeDtypeStruct((rows, terms[0].shape[1]), out_type),
        in_specs=[VMEM] * len(terms) + [HBM] * len(after),
        out_specs=VMEM,
        compiler_params=pltpu.CompilerParams(vmem_limit_bytes=8 << 20),
    )(*terms, *after)


def shards(tokens, expert_ids, gate_weights, w_gate, w_up, w_down):
    tok_rows, model_width = tokens.shape
    groups = lax.axis_size("grp")
    owners = lax.axis_size("exp")
    experts = groups * owners
    chips = owners // CORES
    mine = lax.axis_index("grp") * owners + lax.axis_index("exp")

    def step_to(value, g, s, back=False):
        pairs = [
            (
                (i * chips + j) * CORES + c,
                (partner(i, g, groups) * chips + partner(j, s, chips)) * CORES + c,
            )
            for i in range(groups)
            for j in range(chips)
            for c in range(CORES)
        ]
        return lax.ppermute(value, ("grp", "exp"), [(d, o) for o, d in pairs] if back else pairs)

    def swap(value):
        return lax.ppermute(value, "exp", [(i, i ^ 1) for i in range(owners)])

    place = find_place(mine[None], experts + -experts % LANES)
    own = prepare(place, tokens, expert_ids, gate_weights)
    weights = (w_gate, w_up, w_down)
    width = groups if experts * tok_rows <= WHOLE_ROWS else 1
    order = [0] + list(range(groups - 1, 0, -1))
    direct = 1 if width > 1 else None
    total = None
    for first in range(0, groups, width):
        if first:
            own, total = lax.optimization_barrier((own, total))
        steps = order[first : first + width]
        near = [step_to(own, g, 0) if g else own for g in steps]
        near_other = [swap(piece) for piece in near]
        keys = [(at, s) for at in range(width) for s in range(1, chips)]
        far = pack([step_to(near[at], 0, s) for at, s in keys], *near_other)
        far_other = swap(far)
        near_kept, near_back, *near_alone = expert_rows(
            place, weights, near, near_other, far, alone=direct
        )
        near_alone = [swap(part) for part in near_alone]
        far_kept, far_back = expert_rows(place, weights, [far], [far_other], *near_alone)
        far_back, near_back = swap(far_back), swap(near_back)

        def near_sum(at, terms, after):
            begin = at * tok_rows
            return add_rows(
                begin, tok_rows, jnp.bfloat16, near_kept, near_back, *terms, after=after
            )

        def far_sum(at, s):
            begin = keys.index((at, s)) * tok_rows
            return add_rows(begin, tok_rows, jnp.bfloat16, far_kept, far_back)

        terms, early, second = [], [], []
        if first == 0:
            terms += [part[:tok_rows] for part in (near_kept, near_back)]
        by_chip = {}
        for at, g in reversed(list(enumerate(steps))):
            if at == direct:
                piece = add_rows(at * tok_rows, tok_rows, jnp.bfloat16, near_kept, *near_alone)
                early.append(step_to(piece, g, 0, True))
                second += [step_to(far_sum(at, s), g, s, True) for s in range(1, chips)]
            else:
                by_chip[at] = [step_to(far_sum(at, s), 0, s, True) for s in range(1, chips)]
        terms += early + second
        for at, g in list(enumerate(steps)):
            if at in by_chip:
                piece = by_chip[at]
                terms += [step_to(near_sum(at, piece, early if at == 2 else early + second), g, 0, True)] if g else piece
        for term in terms:
            term = term.astype(jnp.float32)
            total = term if total is None else total + term
    return total


def solution(mesh):
    return jax.shard_map(
        shards,
        mesh=mesh,
        in_specs=(
            P(("rep", "grp", "exp"), None),
            P(("rep", "grp", "exp"), None),
            P(("rep", "grp", "exp"), None),
            P(("grp", "exp"), None, None),
            P(("grp", "exp"), None, None),
            P(("grp", "exp"), None, None),
        ),
        out_specs=P(("rep", "grp", "exp"), None),
        check_vma=False,
    )
```

```python
import functools

import jax
import jax.numpy as jnp
from jax import lax
from jax.experimental import pallas as pl
from jax.experimental.pallas import tpu as pltpu
from jax.sharding import PartitionSpec as P

CORES = 2
LANES = 128
WHOLE_ROWS = 512
PLACE_FLOPS = 1 << 31
PREP_FLOPS = 1 << 35
VMEM = pl.BlockSpec(memory_space=pltpu.VMEM)
SMEM = pl.BlockSpec(memory_space=pltpu.SMEM)
HBM = pl.BlockSpec(memory_space=pltpu.HBM)


def partner(index, step, count):
    return index ^ step if count & (count - 1) == 0 else (index + step) % count


def place_kernel(mine_ref, out_ref):
    out_ref[...] = jnp.zeros_like(out_ref) + mine_ref[0]


def find_place(mine, width):
    return pl.pallas_call(
        place_kernel,
        out_shape=jax.ShapeDtypeStruct((8, width), jnp.int32),
        in_specs=[SMEM],
        out_specs=VMEM,
        compiler_params=pltpu.CompilerParams(vmem_limit_bytes=8 << 20),
        cost_estimate=pl.CostEstimate(flops=PLACE_FLOPS, bytes_accessed=0, transcendentals=0),
    )(mine)


def prep_kernel(place_ref, ids_ref, gates_ref, tokens_ref, out_ref):
    model_width = tokens_ref.shape[1]
    width = out_ref.shape[1] - model_width
    out_ref[:, :model_width] = tokens_ref[...]
    ids = ids_ref[...]
    gates = gates_ref[...].astype(jnp.float32)
    top_count, rows = ids.shape
    expert = lax.broadcasted_iota(jnp.int32, (width, rows), 0)
    turned = jnp.zeros((width, rows), jnp.float32)
    for k in range(top_count):
        turned += jnp.where(ids[k : k + 1, :] == expert, gates[k : k + 1, :], 0.0)
    same = lax.broadcasted_iota(jnp.int32, (rows, rows), 0) == lax.broadcasted_iota(
        jnp.int32, (rows, rows), 1
    )
    table = lax.dot_general(
        same.astype(jnp.bfloat16),
        turned.astype(jnp.bfloat16),
        (((1,), (1,)), ((), ())),
        preferred_element_type=jnp.float32,
    )
    out_ref[:, model_width:] = table.astype(jnp.bfloat16)


def prepare(place, tokens, expert_ids, gate_weights):
    rows, model_width = tokens.shape
    return pl.pallas_call(
        prep_kernel,
        out_shape=jax.ShapeDtypeStruct((rows, model_width + place.shape[1]), jnp.bfloat16),
        in_specs=[HBM] + [VMEM] * 3,
        out_specs=VMEM,
        compiler_params=pltpu.CompilerParams(vmem_limit_bytes=8 << 20),
        cost_estimate=pl.CostEstimate(flops=PREP_FLOPS, bytes_accessed=0, transcendentals=0),
    )(place, expert_ids.T, gate_weights.T, tokens)


def row_scale(place_ref, table):
    table = table.astype(jnp.float32)
    lane = lax.broadcasted_iota(jnp.int32, table.shape, 1)
    return jnp.sum(jnp.where(lane == place_ref[:1, :], table, 0.0), axis=1, keepdims=True)


def activate(gate_pre, up_pre):
    return (gate_pre / (1.0 + jnp.exp(-gate_pre)) * up_pre).astype(jnp.bfloat16)


def join(pieces, out_ref):
    at = 0
    for ref in pieces:
        out_ref[at : at + ref.shape[0], :] = ref[...]
        at += ref.shape[0]


def expert_kernel(count, place_ref, *refs):
    kept_ref, given_ref, held = refs[-3:]
    gate_ref, up_ref, down_ref = refs[count : count + 3]
    rows, model_width = kept_ref.shape
    join(refs[:count], held)
    x = held[:, :model_width]
    scale = row_scale(place_ref, held[:, model_width:])
    gate_pre = jnp.dot(x, gate_ref[0], preferred_element_type=jnp.float32)
    up_pre = jnp.dot(x, up_ref[0], preferred_element_type=jnp.float32)
    hidden = activate(gate_pre, up_pre)
    result = jnp.dot(hidden, down_ref[0], preferred_element_type=jnp.float32) * scale
    kept_ref[...] = result[:rows]
    given_ref[...] = result[rows:].astype(given_ref.dtype)


def expert_rows(place, weights, own, other, *after):
    width = own[0].shape[1]
    _, model_width, hidden_width = weights[0].shape
    count = len(own) + len(other)
    rows = sum(piece.shape[0] for piece in own)
    return pl.pallas_call(
        functools.partial(expert_kernel, count),
        out_shape=[
            jax.ShapeDtypeStruct((rows, model_width), jnp.float32),
            jax.ShapeDtypeStruct((rows, model_width), jnp.bfloat16),
        ],
        in_specs=[VMEM] * (count + 4) + [HBM] * len(after),
        out_specs=[VMEM] * 2,
        scratch_shapes=[pltpu.VMEM((2 * rows, width), jnp.bfloat16)],
        compiler_params=pltpu.CompilerParams(vmem_limit_bytes=16 << 20),
        cost_estimate=pl.CostEstimate(
            flops=12 * rows * model_width * hidden_width,
            bytes_accessed=0,
            transcendentals=2 * rows * hidden_width,
        ),
    )(place, *own, *other, *weights, *after)


def pack_kernel(count, *refs):
    join(refs[:count], refs[-1])


def pack(pieces, *after):
    rows = sum(piece.shape[0] for piece in pieces)
    return pl.pallas_call(
        functools.partial(pack_kernel, len(pieces)),
        out_shape=jax.ShapeDtypeStruct((rows, pieces[0].shape[1]), pieces[0].dtype),
        in_specs=[VMEM] * len(pieces) + [HBM] * len(after),
        out_specs=VMEM,
        compiler_params=pltpu.CompilerParams(vmem_limit_bytes=8 << 20),
    )(*pieces, *after)


def add_kernel(first, *refs):
    out_ref = refs[-1]
    rows = out_ref.shape[0]
    total = None
    for ref in refs[:-1]:
        part = ref[...] if ref.shape[0] == rows else ref[first : first + rows, :]
        part = part.astype(jnp.float32)
        total = part if total is None else total + part
    out_ref[...] = total.astype(out_ref.dtype)


def add_rows(first, rows, out_type, *terms):
    return pl.pallas_call(
        functools.partial(add_kernel, first),
        out_shape=jax.ShapeDtypeStruct((rows, terms[0].shape[1]), out_type),
        in_specs=[VMEM] * len(terms),
        out_specs=VMEM,
        compiler_params=pltpu.CompilerParams(vmem_limit_bytes=8 << 20),
    )(*terms)


def shards(tokens, expert_ids, gate_weights, w_gate, w_up, w_down):
    tok_rows, model_width = tokens.shape
    groups = lax.axis_size("grp")
    owners = lax.axis_size("exp")
    experts = groups * owners
    chips = owners // CORES
    mine = lax.axis_index("grp") * owners + lax.axis_index("exp")

    def step_to(value, g, s, back=False):
        pairs = [
            (
                (i * chips + j) * CORES + c,
                (partner(i, g, groups) * chips + partner(j, s, chips)) * CORES + c,
            )
            for i in range(groups)
            for j in range(chips)
            for c in range(CORES)
        ]
        return lax.ppermute(value, ("grp", "exp"), [(d, o) for o, d in pairs] if back else pairs)

    def swap(value):
        return lax.ppermute(value, "exp", [(i, i ^ 1) for i in range(owners)])

    place = find_place(mine[None], experts + -experts % LANES)
    own = prepare(place, tokens, expert_ids, gate_weights)
    weights = (w_gate, w_up, w_down)
    width = groups if experts * tok_rows <= WHOLE_ROWS else 1
    total = None
    for first in range(0, groups, width):
        if first:
            own, total = lax.optimization_barrier((own, total))
        steps = range(first, first + width)
        near = [step_to(own, g, 0) if g else own for g in steps]
        far = [
            step_to(own, g, s) if g == 1 else step_to(near[at], 0, s)
            for at, g in enumerate(steps)
            for s in range(1, chips)
        ]
        near_other = [swap(piece) for piece in near]
        far_block = pack(far, *near_other)
        near_kept, near_back = expert_rows(
            place, weights, near, near_other, far_block
        )
        far_kept, far_back = expert_rows(place, weights, [far_block], [swap(far_block)], near_kept)
        far_back, near_back = swap(far_back), swap(near_back)

        def near_sum(at, *terms):
            begin = at * tok_rows
            return add_rows(begin, tok_rows, jnp.bfloat16, near_kept, near_back, *terms)

        def far_sum(at, s):
            begin = (at * (chips - 1) + s - 1) * tok_rows
            return add_rows(begin, tok_rows, jnp.bfloat16, far_kept, far_back)

        terms = []
        if first == 0:
            terms += [part[:tok_rows] for part in (near_kept, near_back)]
        by_chip = {
            at: [step_to(far_sum(at, s), 0, s, True) for s in range(1, chips)]
            for at in reversed(range(width))
        }
        for at, g in reversed(list(enumerate(steps))):
            terms += [step_to(near_sum(at, *by_chip[at]), g, 0, True)] if g else by_chip[at]
        for term in terms:
            term = term.astype(jnp.float32)
            total = term if total is None else total + term
    return total


def solution(mesh):
    return jax.shard_map(
        shards,
        mesh=mesh,
        in_specs=(
            P(("rep", "grp", "exp"), None),
            P(("rep", "grp", "exp"), None),
            P(("rep", "grp", "exp"), None),
            P(("grp", "exp"), None, None),
            P(("grp", "exp"), None, None),
            P(("grp", "exp"), None, None),
        ),
        out_specs=P(("rep", "grp", "exp"), None),
        check_vma=False,
    )
```

```python
import functools

import jax
import jax.numpy as jnp
from jax import lax
from jax.experimental import pallas as pl
from jax.experimental.pallas import tpu as pltpu
from jax.sharding import PartitionSpec as P

CORES = 2
LANES = 128
WHOLE_ROWS = 512
PLACE_FLOPS = 1 << 31
PREP_FLOPS = 1 << 35
VMEM = pl.BlockSpec(memory_space=pltpu.VMEM)
SMEM = pl.BlockSpec(memory_space=pltpu.SMEM)
HBM = pl.BlockSpec(memory_space=pltpu.HBM)


def partner(index, step, count):
    return index ^ step if count & (count - 1) == 0 else (index + step) % count


def place_kernel(mine_ref, out_ref):
    out_ref[...] = jnp.zeros_like(out_ref) + mine_ref[0]


def find_place(mine, width):
    return pl.pallas_call(
        place_kernel,
        out_shape=jax.ShapeDtypeStruct((8, width), jnp.int32),
        in_specs=[SMEM],
        out_specs=VMEM,
        compiler_params=pltpu.CompilerParams(vmem_limit_bytes=8 << 20),
        cost_estimate=pl.CostEstimate(flops=PLACE_FLOPS, bytes_accessed=0, transcendentals=0),
    )(mine)


def prep_kernel(place_ref, ids_ref, gates_ref, tokens_ref, out_ref):
    model_width = tokens_ref.shape[1]
    width = out_ref.shape[1] - model_width
    out_ref[:, :model_width] = tokens_ref[...]
    ids = ids_ref[...]
    gates = gates_ref[...].astype(jnp.float32)
    top_count, rows = ids.shape
    expert = lax.broadcasted_iota(jnp.int32, (width, rows), 0)
    turned = jnp.zeros((width, rows), jnp.float32)
    for k in range(top_count):
        turned += jnp.where(ids[k : k + 1, :] == expert, gates[k : k + 1, :], 0.0)
    same = lax.broadcasted_iota(jnp.int32, (rows, rows), 0) == lax.broadcasted_iota(
        jnp.int32, (rows, rows), 1
    )
    table = lax.dot_general(
        same.astype(jnp.bfloat16),
        turned.astype(jnp.bfloat16),
        (((1,), (1,)), ((), ())),
        preferred_element_type=jnp.float32,
    )
    out_ref[:, model_width:] = table.astype(jnp.bfloat16)


def prepare(place, tokens, expert_ids, gate_weights):
    rows, model_width = tokens.shape
    return pl.pallas_call(
        prep_kernel,
        out_shape=jax.ShapeDtypeStruct((rows, model_width + place.shape[1]), jnp.bfloat16),
        in_specs=[HBM] + [VMEM] * 3,
        out_specs=VMEM,
        compiler_params=pltpu.CompilerParams(vmem_limit_bytes=8 << 20),
        cost_estimate=pl.CostEstimate(flops=PREP_FLOPS, bytes_accessed=0, transcendentals=0),
    )(place, expert_ids.T, gate_weights.T, tokens)


def row_scale(place_ref, table):
    table = table.astype(jnp.float32)
    lane = lax.broadcasted_iota(jnp.int32, table.shape, 1)
    return jnp.sum(jnp.where(lane == place_ref[:1, :], table, 0.0), axis=1, keepdims=True)


def activate(gate_pre, up_pre):
    return (gate_pre / (1.0 + jnp.exp(-gate_pre)) * up_pre).astype(jnp.bfloat16)


def join(pieces, out_ref):
    at = 0
    for ref in pieces:
        out_ref[at : at + ref.shape[0], :] = ref[...]
        at += ref.shape[0]


def expert_kernel(count, starts, place_ref, *refs):
    kept_ref, *given_refs, held = refs[-2 - len(starts) :]
    gate_ref, up_ref, down_ref = refs[count : count + 3]
    rows, model_width = kept_ref.shape
    join(refs[:count], held)
    x = held[:, :model_width]
    scale = row_scale(place_ref, held[:, model_width:])
    gate_pre = jnp.dot(x, gate_ref[0], preferred_element_type=jnp.float32)
    up_pre = jnp.dot(x, up_ref[0], preferred_element_type=jnp.float32)
    hidden = activate(gate_pre, up_pre)
    result = jnp.dot(hidden, down_ref[0], preferred_element_type=jnp.float32) * scale
    kept_ref[...] = result[:rows]
    for ref, at in zip(given_refs, starts):
        ref[...] = result[rows + at : rows + at + ref.shape[0]].astype(ref.dtype)


def expert_rows(place, weights, own, other, *after, alone=None):
    width = own[0].shape[1]
    _, model_width, hidden_width = weights[0].shape
    count = len(own) + len(other)
    rows = sum(piece.shape[0] for piece in own)
    starts, parts = [0], [rows]
    if alone is not None:
        starts.append(alone[0])
        parts.append(alone[1])
    return pl.pallas_call(
        functools.partial(expert_kernel, count, starts),
        out_shape=[
            jax.ShapeDtypeStruct((rows, model_width), jnp.float32),
            *[jax.ShapeDtypeStruct((part, model_width), jnp.bfloat16) for part in parts],
        ],
        in_specs=[VMEM] * (count + 4) + [HBM] * len(after),
        out_specs=[VMEM] * (1 + len(parts)),
        scratch_shapes=[pltpu.VMEM((2 * rows, width), jnp.bfloat16)],
        compiler_params=pltpu.CompilerParams(vmem_limit_bytes=16 << 20),
        cost_estimate=pl.CostEstimate(
            flops=12 * rows * model_width * hidden_width,
            bytes_accessed=0,
            transcendentals=2 * rows * hidden_width,
        ),
    )(place, *own, *other, *weights, *after)


def pack_kernel(count, *refs):
    join(refs[:count], refs[-1])


def pack(pieces, *after):
    rows = sum(piece.shape[0] for piece in pieces)
    return pl.pallas_call(
        functools.partial(pack_kernel, len(pieces)),
        out_shape=jax.ShapeDtypeStruct((rows, pieces[0].shape[1]), pieces[0].dtype),
        in_specs=[VMEM] * len(pieces) + [HBM] * len(after),
        out_specs=VMEM,
        compiler_params=pltpu.CompilerParams(vmem_limit_bytes=8 << 20),
    )(*pieces, *after)


def add_kernel(first, *refs):
    out_ref = refs[-1]
    rows = out_ref.shape[0]
    total = None
    for ref in refs[:-1]:
        part = ref[...] if ref.shape[0] == rows else ref[first : first + rows, :]
        part = part.astype(jnp.float32)
        total = part if total is None else total + part
    out_ref[...] = total.astype(out_ref.dtype)


def add_rows(first, rows, out_type, *terms):
    return pl.pallas_call(
        functools.partial(add_kernel, first),
        out_shape=jax.ShapeDtypeStruct((rows, terms[0].shape[1]), out_type),
        in_specs=[VMEM] * len(terms),
        out_specs=VMEM,
        compiler_params=pltpu.CompilerParams(vmem_limit_bytes=8 << 20),
    )(*terms)


def shards(tokens, expert_ids, gate_weights, w_gate, w_up, w_down):
    tok_rows, model_width = tokens.shape
    groups = lax.axis_size("grp")
    owners = lax.axis_size("exp")
    experts = groups * owners
    chips = owners // CORES
    mine = lax.axis_index("grp") * owners + lax.axis_index("exp")

    def step_to(value, g, s, back=False):
        pairs = [
            (
                (i * chips + j) * CORES + c,
                (partner(i, g, groups) * chips + partner(j, s, chips)) * CORES + c,
            )
            for i in range(groups)
            for j in range(chips)
            for c in range(CORES)
        ]
        return lax.ppermute(value, ("grp", "exp"), [(d, o) for o, d in pairs] if back else pairs)

    def swap(value):
        return lax.ppermute(value, "exp", [(i, i ^ 1) for i in range(owners)])

    place = find_place(mine[None], experts + -experts % LANES)
    own = prepare(place, tokens, expert_ids, gate_weights)
    weights = (w_gate, w_up, w_down)
    width = groups if experts * tok_rows <= WHOLE_ROWS else 1
    total = None
    for first in range(0, groups, width):
        if first:
            own, total = lax.optimization_barrier((own, total))
        steps = range(first, first + width)
        near = [step_to(own, g, 0) if g else own for g in steps]
        far = [step_to(piece, 0, s) for piece in near for s in range(1, chips)]
        near_other = [swap(piece) for piece in near]
        far_block = pack(far, *near_other)
        near_kept, near_back = expert_rows(
            place, weights, near, near_other, far_block
        )
        ahead = ((width - 1) * (chips - 1) * tok_rows, tok_rows)
        far_kept, far_back, far_ahead = expert_rows(
            place, weights, [far_block], [swap(far_block)], near_kept, alone=ahead
        )
        far_ahead = swap(far_ahead)
        far_back, near_back = swap(pack([far_back], far_ahead)), swap(near_back)

        def near_sum(at, *terms):
            begin = at * tok_rows
            return add_rows(begin, tok_rows, jnp.bfloat16, near_kept, near_back, *terms)

        def far_sum(at, s):
            begin = (at * (chips - 1) + s - 1) * tok_rows
            back = far_ahead if begin == ahead[0] else far_back
            return add_rows(begin, tok_rows, jnp.bfloat16, far_kept, back)

        terms = []
        if first == 0:
            terms += [part[:tok_rows] for part in (near_kept, near_back)]
        by_chip = {
            at: [step_to(far_sum(at, s), 0, s, True) for s in range(1, chips)]
            for at in reversed(range(width))
        }
        for at, g in reversed(list(enumerate(steps))):
            terms += [step_to(near_sum(at, *by_chip[at]), g, 0, True)] if g else by_chip[at]
        for term in terms:
            term = term.astype(jnp.float32)
            total = term if total is None else total + term
    return total


def solution(mesh):
    return jax.shard_map(
        shards,
        mesh=mesh,
        in_specs=(
            P(("rep", "grp", "exp"), None),
            P(("rep", "grp", "exp"), None),
            P(("rep", "grp", "exp"), None),
            P(("grp", "exp"), None, None),
            P(("grp", "exp"), None, None),
            P(("grp", "exp"), None, None),
        ),
        out_specs=P(("rep", "grp", "exp"), None),
        check_vma=False,
    )
```

```python
import functools

import jax
import jax.numpy as jnp
from jax import lax
from jax.experimental import pallas as pl
from jax.experimental.pallas import tpu as pltpu
from jax.sharding import PartitionSpec as P

CORES = 2
LANES = 128
WHOLE_ROWS = 512
PLACE_FLOPS = 1 << 31
PREP_FLOPS = 1 << 35
VMEM = pl.BlockSpec(memory_space=pltpu.VMEM)
SMEM = pl.BlockSpec(memory_space=pltpu.SMEM)
HBM = pl.BlockSpec(memory_space=pltpu.HBM)


def partner(index, step, count):
    return index ^ step if count & (count - 1) == 0 else (index + step) % count


def place_kernel(mine_ref, out_ref):
    out_ref[...] = jnp.zeros_like(out_ref) + mine_ref[0]


def find_place(mine, width):
    return pl.pallas_call(
        place_kernel,
        out_shape=jax.ShapeDtypeStruct((8, width), jnp.int32),
        in_specs=[SMEM],
        out_specs=VMEM,
        compiler_params=pltpu.CompilerParams(vmem_limit_bytes=8 << 20),
        cost_estimate=pl.CostEstimate(flops=PLACE_FLOPS, bytes_accessed=0, transcendentals=0),
    )(mine)


def prep_kernel(place_ref, ids_ref, gates_ref, tokens_ref, out_ref):
    model_width = tokens_ref.shape[1]
    width = out_ref.shape[1] - model_width
    out_ref[:, :model_width] = tokens_ref[...]
    ids = ids_ref[...]
    gates = gates_ref[...].astype(jnp.float32)
    top_count, rows = ids.shape
    expert = lax.broadcasted_iota(jnp.int32, (width, rows), 0)
    turned = jnp.zeros((width, rows), jnp.float32)
    for k in range(top_count):
        turned += jnp.where(ids[k : k + 1, :] == expert, gates[k : k + 1, :], 0.0)
    same = lax.broadcasted_iota(jnp.int32, (rows, rows), 0) == lax.broadcasted_iota(
        jnp.int32, (rows, rows), 1
    )
    table = lax.dot_general(
        same.astype(jnp.bfloat16),
        turned.astype(jnp.bfloat16),
        (((1,), (1,)), ((), ())),
        preferred_element_type=jnp.float32,
    )
    out_ref[:, model_width:] = table.astype(jnp.bfloat16)


def prepare(place, tokens, expert_ids, gate_weights):
    rows, model_width = tokens.shape
    return pl.pallas_call(
        prep_kernel,
        out_shape=jax.ShapeDtypeStruct((rows, model_width + place.shape[1]), jnp.bfloat16),
        in_specs=[HBM] + [VMEM] * 3,
        out_specs=VMEM,
        compiler_params=pltpu.CompilerParams(vmem_limit_bytes=8 << 20),
        cost_estimate=pl.CostEstimate(flops=PREP_FLOPS, bytes_accessed=0, transcendentals=0),
    )(place, expert_ids.T, gate_weights.T, tokens)


def row_scale(place_ref, table):
    table = table.astype(jnp.float32)
    lane = lax.broadcasted_iota(jnp.int32, table.shape, 1)
    return jnp.sum(jnp.where(lane == place_ref[:1, :], table, 0.0), axis=1, keepdims=True)


def activate(gate_pre, up_pre):
    return (gate_pre / (1.0 + jnp.exp(-gate_pre)) * up_pre).astype(jnp.bfloat16)


def join(pieces, out_ref):
    at = 0
    for ref in pieces:
        out_ref[at : at + ref.shape[0], :] = ref[...]
        at += ref.shape[0]


def expert_kernel(count, place_ref, *refs):
    kept_ref, given_ref, held = refs[-3:]
    gate_ref, up_ref, down_ref = refs[count : count + 3]
    rows, model_width = kept_ref.shape
    join(refs[:count], held)
    x = held[:, :model_width]
    scale = row_scale(place_ref, held[:, model_width:])
    gate_pre = jnp.dot(x, gate_ref[0], preferred_element_type=jnp.float32)
    up_pre = jnp.dot(x, up_ref[0], preferred_element_type=jnp.float32)
    hidden = activate(gate_pre, up_pre)
    result = jnp.dot(hidden, down_ref[0], preferred_element_type=jnp.float32) * scale
    kept_ref[...] = result[:rows]
    given_ref[...] = result[rows:].astype(given_ref.dtype)


def expert_rows(place, weights, own, other, *after):
    width = own[0].shape[1]
    _, model_width, hidden_width = weights[0].shape
    count = len(own) + len(other)
    rows = sum(piece.shape[0] for piece in own)
    return pl.pallas_call(
        functools.partial(expert_kernel, count),
        out_shape=[
            jax.ShapeDtypeStruct((rows, model_width), jnp.float32),
            jax.ShapeDtypeStruct((rows, model_width), jnp.bfloat16),
        ],
        in_specs=[VMEM] * (count + 4) + [HBM] * len(after),
        out_specs=[VMEM] * 2,
        scratch_shapes=[pltpu.VMEM((2 * rows, width), jnp.bfloat16)],
        compiler_params=pltpu.CompilerParams(vmem_limit_bytes=16 << 20),
        cost_estimate=pl.CostEstimate(
            flops=12 * rows * model_width * hidden_width,
            bytes_accessed=0,
            transcendentals=2 * rows * hidden_width,
        ),
    )(place, *own, *other, *weights, *after)


def pack_kernel(count, *refs):
    join(refs[:count], refs[-1])


def pack(pieces, *after):
    rows = sum(piece.shape[0] for piece in pieces)
    return pl.pallas_call(
        functools.partial(pack_kernel, len(pieces)),
        out_shape=jax.ShapeDtypeStruct((rows, pieces[0].shape[1]), pieces[0].dtype),
        in_specs=[VMEM] * len(pieces) + [HBM] * len(after),
        out_specs=VMEM,
        compiler_params=pltpu.CompilerParams(vmem_limit_bytes=8 << 20),
    )(*pieces, *after)


def add_kernel(first, *refs):
    out_ref = refs[-1]
    rows = out_ref.shape[0]
    total = None
    for ref in refs[:-1]:
        part = ref[...] if ref.shape[0] == rows else ref[first : first + rows, :]
        part = part.astype(jnp.float32)
        total = part if total is None else total + part
    out_ref[...] = total.astype(out_ref.dtype)


def add_rows(first, rows, out_type, *terms):
    return pl.pallas_call(
        functools.partial(add_kernel, first),
        out_shape=jax.ShapeDtypeStruct((rows, terms[0].shape[1]), out_type),
        in_specs=[VMEM] * len(terms),
        out_specs=VMEM,
        compiler_params=pltpu.CompilerParams(vmem_limit_bytes=8 << 20),
    )(*terms)


def shards(tokens, expert_ids, gate_weights, w_gate, w_up, w_down):
    tok_rows, model_width = tokens.shape
    groups = lax.axis_size("grp")
    owners = lax.axis_size("exp")
    experts = groups * owners
    chips = owners // CORES
    mine = lax.axis_index("grp") * owners + lax.axis_index("exp")

    def step_to(value, g, s, back=False):
        pairs = [
            (
                (i * chips + j) * CORES + c,
                (partner(i, g, groups) * chips + partner(j, s, chips)) * CORES + c,
            )
            for i in range(groups)
            for j in range(chips)
            for c in range(CORES)
        ]
        return lax.ppermute(value, ("grp", "exp"), [(d, o) for o, d in pairs] if back else pairs)

    def swap(value):
        return lax.ppermute(value, "exp", [(i, i ^ 1) for i in range(owners)])

    place = find_place(mine[None], experts + -experts % LANES)
    own = prepare(place, tokens, expert_ids, gate_weights)
    weights = (w_gate, w_up, w_down)
    width = groups if experts * tok_rows <= WHOLE_ROWS else 1
    order = [*range(groups)]
    order[-2:] = order[:-3:-1]
    total = None
    for first in range(0, groups, width):
        if first:
            own, total = lax.optimization_barrier((own, total))
        steps = order[first : first + width]
        near = [step_to(own, g, 0) if g else own for g in steps]
        far = [step_to(piece, 0, s) for piece in near for s in range(1, chips)]
        near_other = [swap(piece) for piece in near]
        far_block = pack(far, *near_other)
        near_kept, near_back = expert_rows(
            place, weights, near, near_other, far_block
        )
        far_kept, far_back = expert_rows(place, weights, [far_block], [swap(far_block)], near_kept)
        far_back, near_back = swap(far_back), swap(near_back)

        def near_sum(at, *terms):
            begin = at * tok_rows
            return add_rows(begin, tok_rows, jnp.bfloat16, near_kept, near_back, *terms)

        def far_sum(at, s):
            begin = (at * (chips - 1) + s - 1) * tok_rows
            return add_rows(begin, tok_rows, jnp.bfloat16, far_kept, far_back)

        terms = []
        if first == 0:
            terms += [part[:tok_rows] for part in (near_kept, near_back)]
        by_chip = {
            at: [step_to(far_sum(at, s), 0, s, True) for s in range(1, chips)]
            for at in reversed(range(width))
        }
        for at, g in reversed(list(enumerate(steps))):
            terms += [step_to(near_sum(at, *by_chip[at]), g, 0, True)] if g else by_chip[at]
        for term in terms:
            term = term.astype(jnp.float32)
            total = term if total is None else total + term
    return total


def solution(mesh):
    return jax.shard_map(
        shards,
        mesh=mesh,
        in_specs=(
            P(("rep", "grp", "exp"), None),
            P(("rep", "grp", "exp"), None),
            P(("rep", "grp", "exp"), None),
            P(("grp", "exp"), None, None),
            P(("grp", "exp"), None, None),
            P(("grp", "exp"), None, None),
        ),
        out_specs=P(("rep", "grp", "exp"), None),
        check_vma=False,
    )
```

```python
import functools

import jax
import jax.numpy as jnp
from jax import lax
from jax.experimental import pallas as pl
from jax.experimental.pallas import tpu as pltpu
from jax.sharding import PartitionSpec as P

CORES = 2
LANES = 128
WHOLE_ROWS = 512
PLACE_FLOPS = 1 << 31
PREP_FLOPS = 1 << 35
VMEM = pl.BlockSpec(memory_space=pltpu.VMEM)
SMEM = pl.BlockSpec(memory_space=pltpu.SMEM)
HBM = pl.BlockSpec(memory_space=pltpu.HBM)


def partner(index, step, count):
    return index ^ step if count & (count - 1) == 0 else (index + step) % count


def place_kernel(mine_ref, out_ref):
    out_ref[...] = jnp.zeros_like(out_ref) + mine_ref[0]


def find_place(mine, width):
    return pl.pallas_call(
        place_kernel,
        out_shape=jax.ShapeDtypeStruct((8, width), jnp.int32),
        in_specs=[SMEM],
        out_specs=VMEM,
        compiler_params=pltpu.CompilerParams(vmem_limit_bytes=8 << 20),
        cost_estimate=pl.CostEstimate(flops=PLACE_FLOPS, bytes_accessed=0, transcendentals=0),
    )(mine)


def prep_kernel(place_ref, ids_ref, gates_ref, tokens_ref, out_ref):
    model_width = tokens_ref.shape[1]
    width = out_ref.shape[1] - model_width
    out_ref[:, :model_width] = tokens_ref[...]
    ids = ids_ref[...]
    gates = gates_ref[...].astype(jnp.float32)
    top_count, rows = ids.shape
    expert = lax.broadcasted_iota(jnp.int32, (width, rows), 0)
    turned = jnp.zeros((width, rows), jnp.float32)
    for k in range(top_count):
        turned += jnp.where(ids[k : k + 1, :] == expert, gates[k : k + 1, :], 0.0)
    same = lax.broadcasted_iota(jnp.int32, (rows, rows), 0) == lax.broadcasted_iota(
        jnp.int32, (rows, rows), 1
    )
    table = lax.dot_general(
        same.astype(jnp.bfloat16),
        turned.astype(jnp.bfloat16),
        (((1,), (1,)), ((), ())),
        preferred_element_type=jnp.float32,
    )
    out_ref[:, model_width:] = table.astype(jnp.bfloat16)


def prepare(place, tokens, expert_ids, gate_weights):
    rows, model_width = tokens.shape
    return pl.pallas_call(
        prep_kernel,
        out_shape=jax.ShapeDtypeStruct((rows, model_width + place.shape[1]), jnp.bfloat16),
        in_specs=[HBM] + [VMEM] * 3,
        out_specs=VMEM,
        compiler_params=pltpu.CompilerParams(vmem_limit_bytes=8 << 20),
        cost_estimate=pl.CostEstimate(flops=PREP_FLOPS, bytes_accessed=0, transcendentals=0),
    )(place, expert_ids.T, gate_weights.T, tokens)


def row_scale(place_ref, table):
    table = table.astype(jnp.float32)
    lane = lax.broadcasted_iota(jnp.int32, table.shape, 1)
    return jnp.sum(jnp.where(lane == place_ref[:1, :], table, 0.0), axis=1, keepdims=True)


def activate(gate_pre, up_pre):
    return (gate_pre / (1.0 + jnp.exp(-gate_pre)) * up_pre).astype(jnp.bfloat16)


def join(pieces, out_ref):
    at = 0
    for ref in pieces:
        out_ref[at : at + ref.shape[0], :] = ref[...]
        at += ref.shape[0]


def expert_kernel(count, place_ref, *refs):
    kept_ref, given_ref, held = refs[-3:]
    gate_ref, up_ref, down_ref = refs[count : count + 3]
    rows, model_width = kept_ref.shape
    join(refs[:count], held)
    x = held[:, :model_width]
    scale = row_scale(place_ref, held[:, model_width:])
    gate_pre = jnp.dot(x, gate_ref[0], preferred_element_type=jnp.float32)
    up_pre = jnp.dot(x, up_ref[0], preferred_element_type=jnp.float32)
    hidden = activate(gate_pre, up_pre)
    result = jnp.dot(hidden, down_ref[0], preferred_element_type=jnp.float32) * scale
    kept_ref[...] = result[:rows]
    given_ref[...] = result[rows:].astype(given_ref.dtype)


def expert_rows(place, weights, own, other, *after):
    width = own[0].shape[1]
    _, model_width, hidden_width = weights[0].shape
    count = len(own) + len(other)
    rows = sum(piece.shape[0] for piece in own)
    return pl.pallas_call(
        functools.partial(expert_kernel, count),
        out_shape=[
            jax.ShapeDtypeStruct((rows, model_width), jnp.float32),
            jax.ShapeDtypeStruct((rows, model_width), jnp.bfloat16),
        ],
        in_specs=[VMEM] * (count + 4) + [HBM] * len(after),
        out_specs=[VMEM] * 2,
        scratch_shapes=[pltpu.VMEM((2 * rows, width), jnp.bfloat16)],
        compiler_params=pltpu.CompilerParams(vmem_limit_bytes=16 << 20),
        cost_estimate=pl.CostEstimate(
            flops=12 * rows * model_width * hidden_width,
            bytes_accessed=0,
            transcendentals=2 * rows * hidden_width,
        ),
    )(place, *own, *other, *weights, *after)


def pack_kernel(count, *refs):
    join(refs[:count], refs[-1])


def pack(pieces, *after):
    rows = sum(piece.shape[0] for piece in pieces)
    return pl.pallas_call(
        functools.partial(pack_kernel, len(pieces)),
        out_shape=jax.ShapeDtypeStruct((rows, pieces[0].shape[1]), pieces[0].dtype),
        in_specs=[VMEM] * len(pieces) + [HBM] * len(after),
        out_specs=VMEM,
        compiler_params=pltpu.CompilerParams(vmem_limit_bytes=8 << 20),
    )(*pieces, *after)


def add_kernel(first, *refs):
    out_ref = refs[-1]
    rows = out_ref.shape[0]
    total = None
    for ref in refs[:-1]:
        part = ref[...] if ref.shape[0] == rows else ref[first : first + rows, :]
        part = part.astype(jnp.float32)
        total = part if total is None else total + part
    out_ref[...] = total.astype(out_ref.dtype)


def add_rows(first, rows, out_type, *terms):
    return pl.pallas_call(
        functools.partial(add_kernel, first),
        out_shape=jax.ShapeDtypeStruct((rows, terms[0].shape[1]), out_type),
        in_specs=[VMEM] * len(terms),
        out_specs=VMEM,
        compiler_params=pltpu.CompilerParams(vmem_limit_bytes=8 << 20),
    )(*terms)


def shards(tokens, expert_ids, gate_weights, w_gate, w_up, w_down):
    tok_rows, model_width = tokens.shape
    groups = lax.axis_size("grp")
    owners = lax.axis_size("exp")
    experts = groups * owners
    chips = owners // CORES
    mine = lax.axis_index("grp") * owners + lax.axis_index("exp")

    def step_to(value, g, s, back=False):
        pairs = [
            (
                (i * chips + j) * CORES + c,
                (partner(i, g, groups) * chips + partner(j, s, chips)) * CORES + c,
            )
            for i in range(groups)
            for j in range(chips)
            for c in range(CORES)
        ]
        return lax.ppermute(value, ("grp", "exp"), [(d, o) for o, d in pairs] if back else pairs)

    def swap(value):
        return lax.ppermute(value, "exp", [(i, i ^ 1) for i in range(owners)])

    place = find_place(mine[None], experts + -experts % LANES)
    own = prepare(place, tokens, expert_ids, gate_weights)
    weights = (w_gate, w_up, w_down)
    width = groups if experts * tok_rows <= WHOLE_ROWS else 1
    order = [0, *range(groups - 1, 0, -1)]
    total = None
    for first in range(0, groups, width):
        if first:
            own, total = lax.optimization_barrier((own, total))
        steps = order[first : first + width]
        near = [step_to(own, g, 0) if g else own for g in steps]
        far = [step_to(piece, 0, s) for piece in near for s in range(1, chips)]
        near_other = [swap(piece) for piece in near]
        far_block = pack(far, *near_other)
        near_kept, near_back = expert_rows(
            place, weights, near, near_other, far_block
        )
        far_kept, far_back = expert_rows(place, weights, [far_block], [swap(far_block)], near_kept)
        far_back, near_back = swap(far_back), swap(near_back)

        def near_sum(at, *terms):
            begin = at * tok_rows
            return add_rows(begin, tok_rows, jnp.bfloat16, near_kept, near_back, *terms)

        def far_sum(at, s):
            begin = (at * (chips - 1) + s - 1) * tok_rows
            return add_rows(begin, tok_rows, jnp.bfloat16, far_kept, far_back)

        terms = []
        if first == 0:
            terms += [part[:tok_rows] for part in (near_kept, near_back)]
        by_chip, direct = {}, []
        for at, g in reversed(list(enumerate(steps))):
            if g == 1:
                direct.append(step_to(near_sum(at), g, 0, True))
                direct += [step_to(far_sum(at, s), g, s, True) for s in range(1, chips)]
            else:
                by_chip[at] = [step_to(far_sum(at, s), 0, s, True) for s in range(1, chips)]
        terms += direct
        for at, g in reversed(list(enumerate(steps))):
            if at in by_chip:
                terms += [step_to(near_sum(at, *by_chip[at]), g, 0, True)] if g else by_chip[at]
        for term in terms:
            term = term.astype(jnp.float32)
            total = term if total is None else total + term
    return total


def solution(mesh):
    return jax.shard_map(
        shards,
        mesh=mesh,
        in_specs=(
            P(("rep", "grp", "exp"), None),
            P(("rep", "grp", "exp"), None),
            P(("rep", "grp", "exp"), None),
            P(("grp", "exp"), None, None),
            P(("grp", "exp"), None, None),
            P(("grp", "exp"), None, None),
        ),
        out_specs=P(("rep", "grp", "exp"), None),
        check_vma=False,
    )
```

```python
import functools

import jax
import jax.numpy as jnp
from jax import lax
from jax.experimental import pallas as pl
from jax.experimental.pallas import tpu as pltpu
from jax.sharding import PartitionSpec as P

CORES = 2
LANES = 128
WHOLE_ROWS = 512
PLACE_FLOPS = 1 << 31
PREP_FLOPS = 1 << 35
VMEM = pl.BlockSpec(memory_space=pltpu.VMEM)
SMEM = pl.BlockSpec(memory_space=pltpu.SMEM)
HBM = pl.BlockSpec(memory_space=pltpu.HBM)


def partner(index, step, count):
    return index ^ step if count & (count - 1) == 0 else (index + step) % count


def place_kernel(mine_ref, out_ref):
    out_ref[...] = jnp.zeros_like(out_ref) + mine_ref[0]


def find_place(mine, width):
    return pl.pallas_call(
        place_kernel,
        out_shape=jax.ShapeDtypeStruct((8, width), jnp.int32),
        in_specs=[SMEM],
        out_specs=VMEM,
        compiler_params=pltpu.CompilerParams(vmem_limit_bytes=8 << 20),
        cost_estimate=pl.CostEstimate(flops=PLACE_FLOPS, bytes_accessed=0, transcendentals=0),
    )(mine)


def prep_kernel(place_ref, ids_ref, gates_ref, tokens_ref, out_ref):
    model_width = tokens_ref.shape[1]
    width = out_ref.shape[1] - model_width
    out_ref[:, :model_width] = tokens_ref[...]
    ids = ids_ref[...]
    gates = gates_ref[...].astype(jnp.float32)
    top_count, rows = ids.shape
    expert = lax.broadcasted_iota(jnp.int32, (width, rows), 0)
    turned = jnp.zeros((width, rows), jnp.float32)
    for k in range(top_count):
        turned += jnp.where(ids[k : k + 1, :] == expert, gates[k : k + 1, :], 0.0)
    same = lax.broadcasted_iota(jnp.int32, (rows, rows), 0) == lax.broadcasted_iota(
        jnp.int32, (rows, rows), 1
    )
    table = lax.dot_general(
        same.astype(jnp.bfloat16),
        turned.astype(jnp.bfloat16),
        (((1,), (1,)), ((), ())),
        preferred_element_type=jnp.float32,
    )
    out_ref[:, model_width:] = table.astype(jnp.bfloat16)


def prepare(place, tokens, expert_ids, gate_weights):
    rows, model_width = tokens.shape
    return pl.pallas_call(
        prep_kernel,
        out_shape=jax.ShapeDtypeStruct((rows, model_width + place.shape[1]), jnp.bfloat16),
        in_specs=[HBM] + [VMEM] * 3,
        out_specs=VMEM,
        compiler_params=pltpu.CompilerParams(vmem_limit_bytes=8 << 20),
        cost_estimate=pl.CostEstimate(flops=PREP_FLOPS, bytes_accessed=0, transcendentals=0),
    )(place, expert_ids.T, gate_weights.T, tokens)


def row_scale(place_ref, table):
    table = table.astype(jnp.float32)
    lane = lax.broadcasted_iota(jnp.int32, table.shape, 1)
    return jnp.sum(jnp.where(lane == place_ref[:1, :], table, 0.0), axis=1, keepdims=True)


def activate(gate_pre, up_pre):
    return (gate_pre / (1.0 + jnp.exp(-gate_pre)) * up_pre).astype(jnp.bfloat16)


def join(pieces, out_ref):
    at = 0
    for ref in pieces:
        out_ref[at : at + ref.shape[0], :] = ref[...]
        at += ref.shape[0]


def expert_kernel(count, place_ref, *refs):
    kept_ref, given_ref, held = refs[-3:]
    gate_ref, up_ref, down_ref = refs[count : count + 3]
    rows, model_width = kept_ref.shape
    join(refs[:count], held)
    x = held[:, :model_width]
    scale = row_scale(place_ref, held[:, model_width:])
    gate_pre = jnp.dot(x, gate_ref[0], preferred_element_type=jnp.float32)
    up_pre = jnp.dot(x, up_ref[0], preferred_element_type=jnp.float32)
    hidden = activate(gate_pre, up_pre)
    result = jnp.dot(hidden, down_ref[0], preferred_element_type=jnp.float32) * scale
    kept_ref[...] = result[:rows]
    given_ref[...] = result[rows:].astype(given_ref.dtype)


def expert_rows(place, weights, own, other, *after):
    width = own[0].shape[1]
    _, model_width, hidden_width = weights[0].shape
    count = len(own) + len(other)
    rows = sum(piece.shape[0] for piece in own)
    return pl.pallas_call(
        functools.partial(expert_kernel, count),
        out_shape=[
            jax.ShapeDtypeStruct((rows, model_width), jnp.float32),
            jax.ShapeDtypeStruct((rows, model_width), jnp.bfloat16),
        ],
        in_specs=[VMEM] * (count + 4) + [HBM] * len(after),
        out_specs=[VMEM] * 2,
        scratch_shapes=[pltpu.VMEM((2 * rows, width), jnp.bfloat16)],
        compiler_params=pltpu.CompilerParams(vmem_limit_bytes=16 << 20),
        cost_estimate=pl.CostEstimate(
            flops=12 * rows * model_width * hidden_width,
            bytes_accessed=0,
            transcendentals=2 * rows * hidden_width,
        ),
    )(place, *own, *other, *weights, *after)


def pack_kernel(count, *refs):
    join(refs[:count], refs[-1])


def pack(pieces, *after):
    rows = sum(piece.shape[0] for piece in pieces)
    return pl.pallas_call(
        functools.partial(pack_kernel, len(pieces)),
        out_shape=jax.ShapeDtypeStruct((rows, pieces[0].shape[1]), pieces[0].dtype),
        in_specs=[VMEM] * len(pieces) + [HBM] * len(after),
        out_specs=VMEM,
        compiler_params=pltpu.CompilerParams(vmem_limit_bytes=8 << 20),
    )(*pieces, *after)


def add_kernel(first, count, *refs):
    out_ref = refs[-1]
    rows = out_ref.shape[0]
    total = None
    for ref in refs[:count]:
        part = ref[...] if ref.shape[0] == rows else ref[first : first + rows, :]
        part = part.astype(jnp.float32)
        total = part if total is None else total + part
    out_ref[...] = total.astype(out_ref.dtype)


def add_rows(first, rows, out_type, *terms, after=()):
    return pl.pallas_call(
        functools.partial(add_kernel, first, len(terms)),
        out_shape=jax.ShapeDtypeStruct((rows, terms[0].shape[1]), out_type),
        in_specs=[VMEM] * len(terms) + [HBM] * len(after),
        out_specs=VMEM,
        compiler_params=pltpu.CompilerParams(vmem_limit_bytes=8 << 20),
    )(*terms, *after)


def shards(tokens, expert_ids, gate_weights, w_gate, w_up, w_down):
    tok_rows, model_width = tokens.shape
    groups = lax.axis_size("grp")
    owners = lax.axis_size("exp")
    experts = groups * owners
    chips = owners // CORES
    mine = lax.axis_index("grp") * owners + lax.axis_index("exp")

    def step_to(value, g, s, back=False):
        pairs = [
            (
                (i * chips + j) * CORES + c,
                (partner(i, g, groups) * chips + partner(j, s, chips)) * CORES + c,
            )
            for i in range(groups)
            for j in range(chips)
            for c in range(CORES)
        ]
        return lax.ppermute(value, ("grp", "exp"), [(d, o) for o, d in pairs] if back else pairs)

    def swap(value):
        return lax.ppermute(value, "exp", [(i, i ^ 1) for i in range(owners)])

    place = find_place(mine[None], experts + -experts % LANES)
    own = prepare(place, tokens, expert_ids, gate_weights)
    weights = (w_gate, w_up, w_down)
    width = groups if experts * tok_rows <= WHOLE_ROWS else 1
    order = [0, *range(groups - 1, 0, -1)]
    total = None
    for first in range(0, groups, width):
        if first:
            own, total = lax.optimization_barrier((own, total))
        steps = order[first : first + width]
        near = [step_to(own, g, 0) if g else own for g in steps]
        far = [step_to(piece, 0, s) for piece in near for s in range(1, chips)]
        near_other = [swap(piece) for piece in near]
        far_block = pack(far, *near_other)
        near_kept, near_back = expert_rows(
            place, weights, near, near_other, far_block
        )
        far_kept, far_back = expert_rows(place, weights, [far_block], [swap(far_block)], near_kept)
        far_back, near_back = swap(far_back), swap(near_back)

        def near_sum(at, *terms):
            begin = at * tok_rows
            return add_rows(begin, tok_rows, jnp.bfloat16, near_kept, near_back, *terms)

        def far_sum(at, s, after=()):
            begin = (at * (chips - 1) + s - 1) * tok_rows
            return add_rows(begin, tok_rows, jnp.bfloat16, far_kept, far_back, after=after)

        terms = []
        if first == 0:
            terms += [part[:tok_rows] for part in (near_kept, near_back)]
        by_chip, direct = {}, []
        for at, g in reversed(list(enumerate(steps))):
            if g != 1:
                by_chip[at] = [step_to(far_sum(at, s), 0, s, True) for s in range(1, chips)]
        for at, g in reversed(list(enumerate(steps))):
            if g == 1:
                direct.append(step_to(near_sum(at), g, 0, True))
                after = by_chip[1] if 1 in by_chip else ()
                direct += [step_to(far_sum(at, s, after), g, s, True) for s in range(1, chips)]
        terms += direct
        for at, g in reversed(list(enumerate(steps))):
            if at in by_chip:
                terms += [step_to(near_sum(at, *by_chip[at]), g, 0, True)] if g else by_chip[at]
        for term in terms:
            term = term.astype(jnp.float32)
            total = term if total is None else total + term
    return total


def solution(mesh):
    return jax.shard_map(
        shards,
        mesh=mesh,
        in_specs=(
            P(("rep", "grp", "exp"), None),
            P(("rep", "grp", "exp"), None),
            P(("rep", "grp", "exp"), None),
            P(("grp", "exp"), None, None),
            P(("grp", "exp"), None, None),
            P(("grp", "exp"), None, None),
        ),
        out_specs=P(("rep", "grp", "exp"), None),
        check_vma=False,
    )
```

```python
import functools

import jax
import jax.numpy as jnp
from jax import lax
from jax.experimental import pallas as pl
from jax.experimental.pallas import tpu as pltpu
from jax.sharding import PartitionSpec as P

CORES = 2
LANES = 128
WHOLE_ROWS = 512
PLACE_FLOPS = 1 << 31
PREP_FLOPS = 1 << 35
VMEM = pl.BlockSpec(memory_space=pltpu.VMEM)
SMEM = pl.BlockSpec(memory_space=pltpu.SMEM)
HBM = pl.BlockSpec(memory_space=pltpu.HBM)


def partner(index, step, count):
    return index ^ step if count & (count - 1) == 0 else (index + step) % count


def place_kernel(mine_ref, out_ref):
    out_ref[...] = jnp.zeros_like(out_ref) + mine_ref[0]


def find_place(mine, width):
    return pl.pallas_call(
        place_kernel,
        out_shape=jax.ShapeDtypeStruct((8, width), jnp.int32),
        in_specs=[SMEM],
        out_specs=VMEM,
        compiler_params=pltpu.CompilerParams(vmem_limit_bytes=8 << 20),
        cost_estimate=pl.CostEstimate(flops=PLACE_FLOPS, bytes_accessed=0, transcendentals=0),
    )(mine)


def prep_kernel(place_ref, ids_ref, gates_ref, tokens_ref, out_ref):
    model_width = tokens_ref.shape[1]
    width = out_ref.shape[1] - model_width
    out_ref[:, :model_width] = tokens_ref[...]
    ids = ids_ref[...]
    gates = gates_ref[...].astype(jnp.float32)
    top_count, rows = ids.shape
    expert = lax.broadcasted_iota(jnp.int32, (width, rows), 0)
    turned = jnp.zeros((width, rows), jnp.float32)
    for k in range(top_count):
        turned += jnp.where(ids[k : k + 1, :] == expert, gates[k : k + 1, :], 0.0)
    same = lax.broadcasted_iota(jnp.int32, (rows, rows), 0) == lax.broadcasted_iota(
        jnp.int32, (rows, rows), 1
    )
    table = lax.dot_general(
        same.astype(jnp.bfloat16),
        turned.astype(jnp.bfloat16),
        (((1,), (1,)), ((), ())),
        preferred_element_type=jnp.float32,
    )
    out_ref[:, model_width:] = table.astype(jnp.bfloat16)


def prepare(place, tokens, expert_ids, gate_weights):
    rows, model_width = tokens.shape
    return pl.pallas_call(
        prep_kernel,
        out_shape=jax.ShapeDtypeStruct((rows, model_width + place.shape[1]), jnp.bfloat16),
        in_specs=[HBM] + [VMEM] * 3,
        out_specs=VMEM,
        compiler_params=pltpu.CompilerParams(vmem_limit_bytes=8 << 20),
        cost_estimate=pl.CostEstimate(flops=PREP_FLOPS, bytes_accessed=0, transcendentals=0),
    )(place, expert_ids.T, gate_weights.T, tokens)


def row_scale(place_ref, table):
    table = table.astype(jnp.float32)
    lane = lax.broadcasted_iota(jnp.int32, table.shape, 1)
    return jnp.sum(jnp.where(lane == place_ref[:1, :], table, 0.0), axis=1, keepdims=True)


def activate(gate_pre, up_pre):
    return (gate_pre / (1.0 + jnp.exp(-gate_pre)) * up_pre).astype(jnp.bfloat16)


def join(pieces, out_ref):
    at = 0
    for ref in pieces:
        out_ref[at : at + ref.shape[0], :] = ref[...]
        at += ref.shape[0]


def expert_kernel(skip, count, *refs):
    place_ref, *refs = refs[skip:]
    kept_ref, given_ref, held = refs[-3:]
    gate_ref, up_ref, down_ref = refs[count : count + 3]
    rows, model_width = kept_ref.shape
    join(refs[:count], held)
    x = held[:, :model_width]
    scale = row_scale(place_ref, held[:, model_width:])
    gate_pre = jnp.dot(x, gate_ref[0], preferred_element_type=jnp.float32)
    up_pre = jnp.dot(x, up_ref[0], preferred_element_type=jnp.float32)
    hidden = activate(gate_pre, up_pre)
    result = jnp.dot(hidden, down_ref[0], preferred_element_type=jnp.float32) * scale
    kept_ref[...] = result[:rows]
    given_ref[...] = result[rows:].astype(given_ref.dtype)


def expert_rows(place, weights, own, other, *after):
    width = own[0].shape[1]
    _, model_width, hidden_width = weights[0].shape
    count = len(own) + len(other)
    rows = sum(piece.shape[0] for piece in own)
    return pl.pallas_call(
        functools.partial(expert_kernel, len(after), count),
        out_shape=[
            jax.ShapeDtypeStruct((rows, model_width), jnp.float32),
            jax.ShapeDtypeStruct((rows, model_width), jnp.bfloat16),
        ],
        in_specs=[HBM] * len(after) + [VMEM] * (count + 4),
        out_specs=[VMEM] * 2,
        scratch_shapes=[pltpu.VMEM((2 * rows, width), jnp.bfloat16)],
        compiler_params=pltpu.CompilerParams(vmem_limit_bytes=16 << 20),
        cost_estimate=pl.CostEstimate(
            flops=12 * rows * model_width * hidden_width,
            bytes_accessed=0,
            transcendentals=2 * rows * hidden_width,
        ),
    )(*after, place, *own, *other, *weights)


def pack_kernel(count, *refs):
    join(refs[:count], refs[-1])


def pack(pieces, *after):
    rows = sum(piece.shape[0] for piece in pieces)
    return pl.pallas_call(
        functools.partial(pack_kernel, len(pieces)),
        out_shape=jax.ShapeDtypeStruct((rows, pieces[0].shape[1]), pieces[0].dtype),
        in_specs=[VMEM] * len(pieces) + [HBM] * len(after),
        out_specs=VMEM,
        compiler_params=pltpu.CompilerParams(vmem_limit_bytes=8 << 20),
    )(*pieces, *after)


def add_kernel(first, *refs):
    out_ref = refs[-1]
    rows = out_ref.shape[0]
    total = None
    for ref in refs[:-1]:
        part = ref[...] if ref.shape[0] == rows else ref[first : first + rows, :]
        part = part.astype(jnp.float32)
        total = part if total is None else total + part
    out_ref[...] = total.astype(out_ref.dtype)


def add_rows(first, rows, out_type, *terms):
    return pl.pallas_call(
        functools.partial(add_kernel, first),
        out_shape=jax.ShapeDtypeStruct((rows, terms[0].shape[1]), out_type),
        in_specs=[VMEM] * len(terms),
        out_specs=VMEM,
        compiler_params=pltpu.CompilerParams(vmem_limit_bytes=8 << 20),
    )(*terms)


def shards(tokens, expert_ids, gate_weights, w_gate, w_up, w_down):
    tok_rows, model_width = tokens.shape
    groups = lax.axis_size("grp")
    owners = lax.axis_size("exp")
    experts = groups * owners
    chips = owners // CORES
    mine = lax.axis_index("grp") * owners + lax.axis_index("exp")

    def step_to(value, g, s, back=False):
        pairs = [
            (
                (i * chips + j) * CORES + c,
                (partner(i, g, groups) * chips + partner(j, s, chips)) * CORES + c,
            )
            for i in range(groups)
            for j in range(chips)
            for c in range(CORES)
        ]
        return lax.ppermute(value, ("grp", "exp"), [(d, o) for o, d in pairs] if back else pairs)

    def swap(value):
        return lax.ppermute(value, "exp", [(i, i ^ 1) for i in range(owners)])

    place = find_place(mine[None], experts + -experts % LANES)
    own = prepare(place, tokens, expert_ids, gate_weights)
    weights = (w_gate, w_up, w_down)
    width = groups if experts * tok_rows <= WHOLE_ROWS else 1
    total = None
    for first in range(0, groups, width):
        if first:
            own, total = lax.optimization_barrier((own, total))
        steps = range(first, first + width)
        near = [step_to(own, g, 0) if g else own for g in steps]
        far = [step_to(piece, 0, s) for piece in near for s in range(1, chips)]
        near_other = [swap(piece) for piece in near]
        far_block = pack(far, *near_other)
        near_kept, near_back = expert_rows(
            place, weights, near, near_other, far_block
        )
        far_kept, far_back = expert_rows(place, weights, [far_block], [swap(far_block)], near_kept)
        far_back, near_back = swap(far_back), swap(near_back)

        def near_sum(at, *terms):
            begin = at * tok_rows
            return add_rows(begin, tok_rows, jnp.bfloat16, near_kept, near_back, *terms)

        def far_sum(at, s):
            begin = (at * (chips - 1) + s - 1) * tok_rows
            return add_rows(begin, tok_rows, jnp.bfloat16, far_kept, far_back)

        terms = []
        if first == 0:
            terms += [part[:tok_rows] for part in (near_kept, near_back)]
        by_chip = {
            at: [step_to(far_sum(at, s), 0, s, True) for s in range(1, chips)]
            for at in reversed(range(width))
        }
        for at, g in reversed(list(enumerate(steps))):
            terms += [step_to(near_sum(at, *by_chip[at]), g, 0, True)] if g else by_chip[at]
        for term in terms:
            term = term.astype(jnp.float32)
            total = term if total is None else total + term
    return total


def solution(mesh):
    return jax.shard_map(
        shards,
        mesh=mesh,
        in_specs=(
            P(("rep", "grp", "exp"), None),
            P(("rep", "grp", "exp"), None),
            P(("rep", "grp", "exp"), None),
            P(("grp", "exp"), None, None),
            P(("grp", "exp"), None, None),
            P(("grp", "exp"), None, None),
        ),
        out_specs=P(("rep", "grp", "exp"), None),
        check_vma=False,
    )
```
